32 devices in a mesh: dp: 16 (over z, x, core), node: 2 (over y).
Axes of the slice: x: 2, y: 2, z: 4, core: 2. Of those that a mesh axis runs over, the one named last changes fastest.
Arguments:
- hidden_in: bfloat16 [4096, 4096], P(('dp', 'node')), may hold values from -6 to 6
- norm_gain: float32 [4096], replicated, may hold values from 0.1 to 1.9
- key_weight: bfloat16 [4096, 1024], P('dp', 'node'), may hold values from -0.09375 to 0.09375
- value_weight: bfloat16 [4096, 1024], P('dp', 'node'), may hold values from -0.09375 to 0.09375
- queries: bfloat16 [4096, 2048], P('dp', 'node'), may hold values from -240 to 240
- out_cotangent: bfloat16 [4096, 2048], P('dp', 'node'), may hold values from -6 to 6
Outputs:
- attention: bfloat16 [4096, 2048], P('dp', 'node')
- key_grad: float32 [4096, 1024], P('dp', 'node')
The draws below stay inside these ranges and needn't reach their ends.
All inputs are finite; a program needn't handle non-finite values.
Results may differ from the reference program's by a relative error of at most 0.0065.
The reference program's roundings to bfloat16 on the way (of `normed`, `probabilities`, `score_grad` and `key_rows_grad`) count: a program that leaves them out, or rounds other values in their place, can miss the bound.
Values may be sent and summed in bfloat16 or wider, within the bound.
A program may use at most 64 MiB of HBM per device.

```python
import jax
import jax.numpy as jnp
from jax import lax

D = 4096
HEADS = 16
KV_HEADS = 8
HD = 128
TOKENS = 4096
N_DP = 16


def draw_queries(key, part):
    key = jax.random.fold_in(key, 7)
    values = jnp.clip(jax.random.normal(jax.random.fold_in(key, 1), (TOKENS, HEADS * HD), jnp.float32), -6.0, 6.0)
    return values.astype(jnp.bfloat16)


def strengthened(entries, own_key, source, target, blocks, factor):
    owner, partner = [(jnp.arange(entries.shape[position]) // (entries.shape[position] // blocks)).reshape([-1 if axis == position else 1 for axis in range(entries.ndim)]) for position in (source, target)]
    chosen = jax.random.permutation(own_key, blocks)[partner]
    strong = (owner == chosen) | (owner == (partner + blocks // 2) % blocks)
    return jnp.where(strong, factor * entries, entries)


def steps_of(stream_key, shape, cuts, smallest, top_value):
    level, own = 1.0, jax.random.fold_in(stream_key, 6)
    for dim, shards_of in cuts:
        steps = jnp.exp(jax.random.uniform(jax.random.fold_in(own, dim), (shards_of,), jnp.float32, smallest / len(cuts), top_value / len(cuts)))
        level = level * jnp.repeat(steps, shape[dim] // shards_of).reshape([-1 if axis == dim else 1 for axis in range(len(shape))])
    return level


def bell_draw(stream_key, shape, spread, reach, split=(), kind=jnp.bfloat16):
    values = spread * jax.random.normal(stream_key, shape, jnp.float32)
    if split:
        values = values * steps_of(stream_key, shape, split, -0.22, 0.18)
    return jnp.clip(values, -reach, reach).astype(kind)


def heavy_noise(rng, shape, spread, limit, cuts, heavy, held_as=jnp.bfloat16):
    drawn = spread * jax.random.normal(rng, shape, jnp.float32)
    if cuts:
        drawn = drawn * steps_of(rng, shape, cuts, -0.22, 0.18)
    return jnp.clip(strengthened(drawn, jax.random.fold_in(rng, 3), *heavy), -limit, limit).astype(held_as)


def setup_inputs(seed: int = 0) -> dict:
    key_list = jax.random.split(jax.random.key(seed), 7)
    hidden_in = heavy_noise(key_list[0], (TOKENS, D), 1.0, 6.0, ((0, 32),), (0, 1, 32, 2.75))
    norm_gain = jnp.clip(1.0 + 0.18 * jax.random.normal(key_list[1], (D,), jnp.float32), 0.1, 1.9)
    key_weight = bell_draw(key_list[2], (D, KV_HEADS * HD), D ** -0.5, 0.09375, ((0, 16), (1, 2)))
    value_weight = bell_draw(key_list[3], (D, KV_HEADS * HD), D ** -0.5, 0.09375, ((0, 16), (1, 2)))
    queries = draw_queries(jax.random.fold_in(key_list[6], 71), 0)
    out_cotangent = bell_draw(key_list[5], (TOKENS, HEADS * HD), 1.0, 6.0, ((0, 16), (1, 2)))
    return {"hidden_in": hidden_in, "norm_gain": norm_gain, "key_weight": key_weight, "value_weight": value_weight, "queries": queries, "out_cotangent": out_cotangent}


epsilon = 1e-05

def rms_normalize(hidden_rows, norm_gain):
    widened = hidden_rows.astype(jnp.float32)
    inverse = lax.rsqrt(lax.optimization_barrier(jnp.mean(widened * widened, axis=-1, keepdims=True)) + epsilon)
    return (widened * inverse * norm_gain.astype(jnp.float32)).astype(jnp.bfloat16)

def one_sequence(key_weight, value_weight, norm_gain, hidden_rows, query_rows, cotangent_rows):
    seq_rows = hidden_rows.shape[0]
    group_size = HEADS // KV_HEADS
    score_scale = HD ** (-0.5)
    normed = rms_normalize(hidden_rows, norm_gain)
    key_proj = jnp.dot(normed, key_weight, preferred_element_type=jnp.float32).astype(jnp.bfloat16)
    value_proj = jnp.dot(normed, value_weight, preferred_element_type=jnp.float32).astype(jnp.bfloat16)
    key_heads = key_proj.reshape(seq_rows, KV_HEADS, HD).astype(jnp.float32)
    value_heads = value_proj.reshape(seq_rows, KV_HEADS, HD).astype(jnp.float32)
    query_heads = query_rows.reshape(seq_rows, KV_HEADS, group_size, HD).astype(jnp.float32)
    grad_heads = cotangent_rows.reshape(seq_rows, KV_HEADS, group_size, HD).astype(jnp.float32)
    scores = jnp.einsum('qkgd,skd->kgqs', query_heads, key_heads) * score_scale
    positions = jnp.arange(seq_rows, dtype=jnp.int32)
    allowed = positions[:, None] >= positions[None, :]
    scores = jnp.where(allowed, scores, -1e+30)
    row_max = lax.optimization_barrier(jnp.max(scores, axis=-1, keepdims=True))
    weights = jnp.exp(scores - row_max)
    probabilities = (weights / lax.optimization_barrier(jnp.sum(weights, axis=-1, keepdims=True))).astype(jnp.bfloat16)
    prob_wide = probabilities.astype(jnp.float32)
    attended = jnp.einsum('kgqs,skd->qkgd', prob_wide, value_heads).astype(jnp.bfloat16)
    prob_grad = jnp.einsum('qkgd,skd->kgqs', grad_heads, value_heads)
    row_delta = lax.optimization_barrier(jnp.sum(prob_wide * prob_grad, axis=-1, keepdims=True))
    score_grad = (prob_wide * (prob_grad - row_delta) * score_scale).astype(jnp.bfloat16)
    key_rows_grad = jnp.einsum('kgqs,qkgd->skd', score_grad.astype(jnp.float32), query_heads)
    key_rows_grad = key_rows_grad.astype(jnp.bfloat16).reshape(seq_rows, KV_HEADS * HD)
    weight_term = jnp.dot(normed.T, key_rows_grad, preferred_element_type=jnp.float32)
    return (attended.reshape(seq_rows, HEADS * HD), weight_term)

def reference(hidden_in, norm_gain, key_weight, value_weight, queries, out_cotangent):
    seq_count = N_DP
    seq_rows = TOKENS // N_DP
    hidden_seq = hidden_in.reshape(seq_count, seq_rows, D)
    query_seq = queries.reshape(seq_count, seq_rows, HEADS * HD)
    grad_seq = out_cotangent.reshape(seq_count, seq_rows, HEADS * HD)

    def advance(running, sliced):
        attended, weight_term = one_sequence(key_weight, value_weight, norm_gain, sliced[0], sliced[1], sliced[2])
        return (running + weight_term, attended)
    key_grad, attended = lax.scan(advance, jnp.zeros((D, KV_HEADS * HD), jnp.float32), (hidden_seq, query_seq, grad_seq))
    return (attended.reshape(TOKENS, HEADS * HD), key_grad)
```

```python
import functools

import jax
import jax.numpy as jnp
from jax import lax
from jax.experimental import pallas as pl
from jax.experimental.pallas import tpu as pltpu
from jax.sharding import PartitionSpec as P

HEADS = 16
KV_HEADS = 8
HD = 128


epsilon = 1e-05


def rms_normalize(hidden_rows, norm_gain):
    widened = hidden_rows.astype(jnp.float32)
    inverse = lax.rsqrt(jnp.mean(widened * widened, axis=-1, keepdims=True) + epsilon)
    return (widened * inverse * norm_gain).astype(jnp.bfloat16)


def local(hidden_in, norm_gain, key_weight, value_weight, queries, out_cotangent):
    local_width = key_weight.shape[1]
    kv_local = local_width // HD
    group_size = HEADS // KV_HEADS
    score_scale = HD ** (-0.5)
    gathered = lax.all_gather(hidden_in, "node", axis=0, tiled=True)
    normed = rms_normalize(gathered, norm_gain)
    seq_rows = normed.shape[0]

    def add_rows(shard_piece):
        return jnp.dot(normed, shard_piece, preferred_element_type=jnp.float32)

    key_sum = add_rows(lax.all_gather(key_weight, "dp", axis=0, tiled=True))
    value_sum = add_rows(lax.all_gather(value_weight, "dp", axis=0, tiled=True))
    key_proj = key_sum.astype(jnp.bfloat16).reshape(seq_rows, kv_local, HD)
    value_proj = value_sum.astype(jnp.bfloat16).reshape(seq_rows, kv_local, HD)
    block_rows = min(512, seq_rows)
    outputs = []
    grad_parts = []
    for block_index in range(seq_rows // block_rows):
        row_start = block_index * block_rows
        span_end = row_start + block_rows
        query_block = queries[row_start:span_end].reshape(block_rows, kv_local, group_size, HD)
        grad_block = out_cotangent[row_start:span_end].reshape(block_rows, kv_local, group_size, HD)
        key_window = key_proj[:span_end]
        value_window = value_proj[:span_end]
        scores = (
            jnp.einsum(
                "qkgd,skd->kgqs", query_block, key_window, preferred_element_type=jnp.float32
            )
            * score_scale
        )
        query_pos = row_start + jnp.arange(block_rows, dtype=jnp.int32)
        key_pos = jnp.arange(span_end, dtype=jnp.int32)
        allowed = query_pos[:, None] >= key_pos[None, :]
        scores = jnp.where(allowed, scores, -1e30)
        row_max = jnp.max(scores, axis=-1, keepdims=True)
        weights = jnp.exp(scores - row_max)
        probabilities = (weights / jnp.sum(weights, axis=-1, keepdims=True)).astype(jnp.bfloat16)
        attended = jnp.einsum(
            "kgqs,skd->qkgd", probabilities, value_window, preferred_element_type=jnp.float32
        )
        outputs.append(
            attended.astype(jnp.bfloat16).reshape(block_rows, kv_local * group_size * HD)
        )
        prob_grad = jnp.einsum(
            "qkgd,skd->kgqs", grad_block, value_window, preferred_element_type=jnp.float32
        )
        row_delta = jnp.sum(probabilities * prob_grad, axis=-1, keepdims=True)
        score_grad = (probabilities * (prob_grad - row_delta) * score_scale).astype(jnp.bfloat16)
        block_grad = jnp.einsum(
            "kgqs,qkgd->skd", score_grad, query_block, preferred_element_type=jnp.float32
        )
        grad_parts.append(jnp.pad(block_grad, ((0, seq_rows - span_end), (0, 0), (0, 0))))
    key_grad_acc = grad_parts[0]
    for extra_part in grad_parts[1:]:
        key_grad_acc = key_grad_acc + extra_part
    key_rows_grad = key_grad_acc.reshape(seq_rows, local_width).astype(jnp.bfloat16)
    key_grad = lax.psum_scatter(
        lax.dot_general(
            normed, key_rows_grad, (((0,), (0,)), ((), ())), preferred_element_type=jnp.float32
        ),
        "dp",
        scatter_dimension=0,
        tiled=True,
    )
    return (jnp.concatenate(outputs, axis=0), key_grad)


SUBS = 2
EARLY = 5


def dot(a, b):
    return jnp.dot(a, b, preferred_element_type=jnp.float32)


def dot_nt(a, b):
    return lax.dot_general(a, b, (((1,), (1,)), ((), ())), preferred_element_type=jnp.float32)


def dot_tn(a, b):
    return lax.dot_general(a, b, (((0,), (0,)), ((), ())), preferred_element_type=jnp.float32)


def kernel(ring, hidden, gain, kw, vw, queries, cotangent, attention, key_grad,
           stage, act, slots, acc, part, kv, rows_grad, sums,
           ag_send, ag_recv, act_send, act_recv, act_local, pair_send, pair_recv,
           rs_send, rs_recv):
    depth = ring // 2
    steps = ring - 1
    dp = lax.axis_index("dp")
    node = lax.axis_index("node")
    core = dp % 2
    block = dp // 2
    col = block % 2
    row = block // 2
    spot = row * (1 - col) + (2 * depth - 1 - row) * col

    def block_at(position):
        position = (position + 2 * ring) % ring
        side = position // depth
        level = position * (1 - side) + (2 * depth - 1 - position) * side
        return level * 2 + side

    right = (block_at(spot + 1) * 2 + core, node)
    left = (block_at(spot - 1) * 2 + core, node)
    sibling = (block * 2 + 1 - core, node)
    beside = (dp, 1 - node)
    across = (block * 2 + 1 - core, 1 - node)
    mesh_ids = pl.DeviceIdType.MESH

    barrier = pltpu.get_barrier_semaphore()
    for peer in (right, left, sibling, beside, across):
        pl.semaphore_signal(barrier, inc=1, device_id=peer, device_id_type=mesh_ids)
    pl.semaphore_wait(barrier, 5)

    def remote(source, target, send, recv, peer):
        copy = pltpu.make_async_remote_copy(
            src_ref=source, dst_ref=target, send_sem=send, recv_sem=recv,
            device_id=peer, device_id_type=mesh_ids)
        copy.start()
        return copy

    onward = (right, left)
    features = kw.shape[0]
    width = kw.shape[1]
    cut = features // SUBS
    started = []

    def gather_copy(way, step, sub):
        span = pl.ds(sub * cut, cut)
        source = (kw, vw)[way].at[span] if step == 0 else slots.at[way, step - 1, span]
        return remote(source, slots.at[way, step, span], ag_send.at[way, step, sub],
                      ag_recv.at[way, step, sub], onward[way])

    flight = {}
    for sub in range(SUBS):
        for way in range(2):
            flight[way, 0, sub] = gather_copy(way, 0, sub)

    own_rows = hidden.shape[0]
    seq = 2 * own_rows
    strip = 16

    def normalize(index, carry):
        rows = pl.ds(pl.multiple_of(index * strip, strip), strip)
        wide = hidden[rows, :].astype(jnp.float32)
        inverse = lax.rsqrt(jnp.mean(wide * wide, axis=-1, keepdims=True) + epsilon)
        normed = (wide * inverse * gain[...]).astype(jnp.bfloat16)
        for piece in range(2 * ring):
            stage[piece % 2, piece // 2, rows, :] = normed[:, piece * features:(piece + 1) * features]
        return carry

    lax.fori_loop(0, own_rows // strip, normalize, 0)
    my_rows = pl.ds(pl.multiple_of(core * seq + node * own_rows, own_rows), own_rows)
    act_copies = []
    for relation, (peer, plane) in enumerate(((across, 1 - core), (beside, core), (sibling, 1 - core))):
        act_copies.append(remote(stage.at[plane], act.at[:, my_rows, :], act_send.at[relation],
                                 act_recv.at[relation], peer))
    local_copy = pltpu.make_async_copy(stage.at[core], act.at[:, my_rows, :], act_local)
    local_copy.start()

    def add_block(way, position, weight):
        acc[way] = acc[way] + dot(act[block_at(position)], weight)

    for step in range(1, steps + 1):
        for sub in range(SUBS):
            for way in range(2):
                flight[way, step - 1, sub].wait_recv()
                if step < steps:
                    flight[way, step, sub] = gather_copy(way, step, sub)
        if step == EARLY:
            local_copy.wait()
            for copy in act_copies:
                copy.wait_recv()
            acc[0] = dot(act[block], kw[...])
            acc[1] = dot(act[block], vw[...])

            def earlier(index, carry):
                add_block(0, spot - 1 - index, slots[0, index])
                add_block(1, spot + 1 + index, slots[1, index])
                return carry

            lax.fori_loop(0, EARLY, earlier, 0)
        if step > EARLY:
            add_block(0, spot - step, slots[0, step - 1])
            add_block(1, spot + step, slots[1, step - 1])

    mine = pl.ds(pl.multiple_of(core * seq, seq), seq)
    theirs = pl.ds(pl.multiple_of((1 - core) * seq, seq), seq)
    pair = remote(acc.at[:, theirs, :], part, pair_send.at[0], pair_recv.at[0], sibling)
    pair.wait_recv()
    kv_heads = width // HD
    group = HEADS // KV_HEADS
    for kind in range(2):
        total = (acc[kind, mine, :] + part[kind]).astype(jnp.bfloat16)
        for head in range(kv_heads):
            kv[kind, head] = total[:, head * HD:(head + 1) * HD]

    scale = HD ** (-0.5)
    allowed = (lax.broadcasted_iota(jnp.int32, (seq, seq), 0)
               >= lax.broadcasted_iota(jnp.int32, (seq, seq), 1))

    def attend(head, carry):
        keys = kv[0, head]
        values = kv[1, head]
        gradient = None
        for member in range(group):
            lanes = pl.ds(pl.multiple_of((head * group + member) * HD, HD), HD)
            query = queries[:, lanes]
            scores = jnp.where(allowed, dot_nt(query, keys) * scale, -1e30)
            weights = jnp.exp(scores - jnp.max(scores, axis=-1, keepdims=True))
            probs = (weights / jnp.sum(weights, axis=-1, keepdims=True)).astype(jnp.bfloat16)
            attention[:, lanes] = dot(probs, values).astype(jnp.bfloat16)
            prob_grad = dot_nt(cotangent[:, lanes], values)
            wide = probs.astype(jnp.float32)
            delta = jnp.sum(wide * prob_grad, axis=-1, keepdims=True)
            score_grad = (wide * (prob_grad - delta) * scale).astype(jnp.bfloat16)
            term = dot_tn(score_grad, query)
            gradient = term if gradient is None else gradient + term
        rows_grad[mine, pl.ds(pl.multiple_of(head * HD, HD), HD)] = gradient.astype(jnp.bfloat16)
        return carry

    lax.fori_loop(0, kv_heads, attend, 0)
    swap = remote(rows_grad.at[mine], rows_grad.at[mine], pair_send.at[1], pair_recv.at[1], sibling)
    swap.wait_recv()

    half = width // 2

    def term_of(way, position):
        return dot_tn(act[block_at(position)], rows_grad[:, way * half:(way + 1) * half])

    ring_flight = {}
    for step in range(steps):
        terms = (term_of(0, spot - 1 - step), term_of(1, spot + 1 + step))
        for sub in range(SUBS):
            span = pl.ds(sub * cut, cut)
            for way in range(2):
                value = terms[way][sub * cut:(sub + 1) * cut]
                if step == 0:
                    sums[way, 0, span, :] = value
                else:
                    ring_flight[way, step - 1, sub].wait_recv()
                    sums[way, step, span, :] = sums[way, step, span, :] + value
                ring_flight[way, step, sub] = remote(
                    sums.at[way, step, span], sums.at[way, step + 1, span],
                    rs_send.at[way, step, sub], rs_recv.at[way, step, sub], onward[way])
    terms = (term_of(0, spot), term_of(1, spot))
    for sub in range(SUBS):
        span = pl.ds(sub * cut, cut)
        for way in range(2):
            ring_flight[way, steps - 1, sub].wait_recv()
            key_grad[span, way * half:(way + 1) * half] = (
                sums[way, steps, span, :] + terms[way][sub * cut:(sub + 1) * cut])
    for copy in [*flight.values(), *act_copies, pair, swap, *ring_flight.values()]:
        copy.wait_send()


def fused(ring, hidden_in, norm_gain, key_weight, value_weight, queries, out_cotangent):
    features, width = key_weight.shape
    own_rows = hidden_in.shape[0]
    seq = 2 * own_rows
    tokens = 2 * seq
    steps = ring - 1
    dma = pltpu.SemaphoreType.DMA
    vmem = pl.BlockSpec(memory_space=pltpu.VMEM)
    return pl.pallas_call(
        functools.partial(kernel, ring),
        out_shape=(
            jax.ShapeDtypeStruct(queries.shape, jnp.bfloat16),
            jax.ShapeDtypeStruct((features, width), jnp.float32),
        ),
        in_specs=[vmem] * 6,
        out_specs=(vmem, vmem),
        scratch_shapes=[
            pltpu.VMEM((2, ring, own_rows, features), jnp.bfloat16),
            pltpu.VMEM((ring, tokens, features), jnp.bfloat16),
            pltpu.VMEM((2, steps, features, width), jnp.bfloat16),
            pltpu.VMEM((2, tokens, width), jnp.float32),
            pltpu.VMEM((2, seq, width), jnp.float32),
            pltpu.VMEM((2, width // HD, seq, HD), jnp.bfloat16),
            pltpu.VMEM((tokens, width), jnp.bfloat16),
            pltpu.VMEM((2, ring, features, width // 2), jnp.float32),
            dma((2, steps, SUBS)),
            dma((2, steps, SUBS)),
            dma((3,)),
            dma((3,)),
            dma,
            dma((2,)),
            dma((2,)),
            dma((2, steps, SUBS)),
            dma((2, steps, SUBS)),
        ],
        compiler_params=pltpu.CompilerParams(
            collective_id=0, has_side_effects=True, vmem_limit_bytes=48 * 1024 * 1024
        ),
        cost_estimate=pl.CostEstimate(flops=4 * 10**9, bytes_accessed=4 * 10**6, transcendentals=0),
    )(hidden_in, norm_gain.reshape(1, -1), key_weight, value_weight, queries, out_cotangent)


def shard_body(mesh, hidden_in, norm_gain, key_weight, value_weight, queries, out_cotangent):
    dp, node = mesh.shape["dp"], mesh.shape["node"]
    features, width = key_weight.shape
    own_rows = hidden_in.shape[0]
    if (
        node == 2
        and dp % 4 == 0
        and EARLY < dp // 2
        and features % 256 == 0
        and width % 256 == 0
        and own_rows % 16 == 0
        and queries.shape[0] == 2 * own_rows
        and own_rows <= 256
    ):
        return fused(dp // 2, hidden_in, norm_gain, key_weight, value_weight, queries, out_cotangent)
    return local(hidden_in, norm_gain, key_weight, value_weight, queries, out_cotangent)


def solution(mesh):
    in_specs = (
        P(("dp", "node"), None),
        P(),
        P("dp", "node"),
        P("dp", "node"),
        P("dp", "node"),
        P("dp", "node"),
    )
    out_specs = (P("dp", "node"), P("dp", "node"))
    return jax.shard_map(functools.partial(shard_body, mesh), mesh=mesh, in_specs=in_specs, out_specs=out_specs, check_vma=False)
```

```python
import functools

import jax
import jax.numpy as jnp
from jax import lax
from jax.experimental import pallas as pl
from jax.experimental.pallas import tpu as pltpu
from jax.sharding import PartitionSpec as P

HEADS = 16
KV_HEADS = 8
HD = 128


epsilon = 1e-05


def rms_normalize(hidden_rows, norm_gain):
    widened = hidden_rows.astype(jnp.float32)
    inverse = lax.rsqrt(jnp.mean(widened * widened, axis=-1, keepdims=True) + epsilon)
    return (widened * inverse * norm_gain).astype(jnp.bfloat16)


def local(hidden_in, norm_gain, key_weight, value_weight, queries, out_cotangent):
    local_width = key_weight.shape[1]
    kv_local = local_width // HD
    group_size = HEADS // KV_HEADS
    score_scale = HD ** (-0.5)
    gathered = lax.all_gather(hidden_in, "node", axis=0, tiled=True)
    normed = rms_normalize(gathered, norm_gain)
    seq_rows = normed.shape[0]

    def add_rows(shard_piece):
        return jnp.dot(normed, shard_piece, preferred_element_type=jnp.float32)

    key_sum = add_rows(lax.all_gather(key_weight, "dp", axis=0, tiled=True))
    value_sum = add_rows(lax.all_gather(value_weight, "dp", axis=0, tiled=True))
    key_proj = key_sum.astype(jnp.bfloat16).reshape(seq_rows, kv_local, HD)
    value_proj = value_sum.astype(jnp.bfloat16).reshape(seq_rows, kv_local, HD)
    block_rows = min(512, seq_rows)
    outputs = []
    grad_parts = []
    for block_index in range(seq_rows // block_rows):
        row_start = block_index * block_rows
        span_end = row_start + block_rows
        query_block = queries[row_start:span_end].reshape(block_rows, kv_local, group_size, HD)
        grad_block = out_cotangent[row_start:span_end].reshape(block_rows, kv_local, group_size, HD)
        key_window = key_proj[:span_end]
        value_window = value_proj[:span_end]
        scores = (
            jnp.einsum(
                "qkgd,skd->kgqs", query_block, key_window, preferred_element_type=jnp.float32
            )
            * score_scale
        )
        query_pos = row_start + jnp.arange(block_rows, dtype=jnp.int32)
        key_pos = jnp.arange(span_end, dtype=jnp.int32)
        allowed = query_pos[:, None] >= key_pos[None, :]
        scores = jnp.where(allowed, scores, -1e30)
        row_max = jnp.max(scores, axis=-1, keepdims=True)
        weights = jnp.exp(scores - row_max)
        probabilities = (weights / jnp.sum(weights, axis=-1, keepdims=True)).astype(jnp.bfloat16)
        attended = jnp.einsum(
            "kgqs,skd->qkgd", probabilities, value_window, preferred_element_type=jnp.float32
        )
        outputs.append(
            attended.astype(jnp.bfloat16).reshape(block_rows, kv_local * group_size * HD)
        )
        prob_grad = jnp.einsum(
            "qkgd,skd->kgqs", grad_block, value_window, preferred_element_type=jnp.float32
        )
        row_delta = jnp.sum(probabilities * prob_grad, axis=-1, keepdims=True)
        score_grad = (probabilities * (prob_grad - row_delta) * score_scale).astype(jnp.bfloat16)
        block_grad = jnp.einsum(
            "kgqs,qkgd->skd", score_grad, query_block, preferred_element_type=jnp.float32
        )
        grad_parts.append(jnp.pad(block_grad, ((0, seq_rows - span_end), (0, 0), (0, 0))))
    key_grad_acc = grad_parts[0]
    for extra_part in grad_parts[1:]:
        key_grad_acc = key_grad_acc + extra_part
    key_rows_grad = key_grad_acc.reshape(seq_rows, local_width).astype(jnp.bfloat16)
    key_grad = lax.psum_scatter(
        lax.dot_general(
            normed, key_rows_grad, (((0,), (0,)), ((), ())), preferred_element_type=jnp.float32
        ),
        "dp",
        scatter_dimension=0,
        tiled=True,
    )
    return (jnp.concatenate(outputs, axis=0), key_grad)


SUBS = 2
EARLY_B = 2


def dot(a, b):
    return jnp.dot(a, b, preferred_element_type=jnp.float32)


def dot_nt(a, b):
    return lax.dot_general(a, b, (((1,), (1,)), ((), ())), preferred_element_type=jnp.float32)


def dot_tn(a, b):
    return lax.dot_general(a, b, (((0,), (0,)), ((), ())), preferred_element_type=jnp.float32)


def kernel(ring, hidden_in, gain, kw, vw, queries_in, cotangent_in, attention, key_grad,
           hidden, own, queries, cotangent, stage, act, slots, acc, part, kv, rows_grad, sums, terms,
           in_sem, ag_send, ag_recv, act_send, act_recv, act_local, pair_send, pair_recv,
           swap_send, swap_recv, rs_send, rs_recv):
    depth = ring // 2
    steps = ring - 1
    dp = lax.axis_index("dp")
    node = lax.axis_index("node")
    core = dp % 2
    block = dp // 2
    col = block % 2
    row = block // 2
    spot = row * (1 - col) + (2 * depth - 1 - row) * col

    def block_at(position):
        position = (position + 2 * ring) % ring
        side = position // depth
        level = position * (1 - side) + (2 * depth - 1 - position) * side
        return level * 2 + side

    def position_of(way, step):
        return spot - step if way == 0 else spot + step

    right = (block_at(spot + 1) * 2 + core, node)
    left = (block_at(spot - 1) * 2 + core, node)
    sibling = (block * 2 + 1 - core, node)
    beside = (dp, 1 - node)
    across = (block * 2 + 1 - core, 1 - node)
    mesh_ids = pl.DeviceIdType.MESH

    loads = [
        pltpu.make_async_copy(hidden_in, hidden, in_sem.at[0]),
        pltpu.make_async_copy(kw, own.at[0], in_sem.at[1]),
        pltpu.make_async_copy(vw, own.at[1], in_sem.at[2]),
        pltpu.make_async_copy(queries_in, queries, in_sem.at[3]),
        pltpu.make_async_copy(cotangent_in, cotangent, in_sem.at[4]),
    ]
    for load in loads:
        load.start()

    barrier = pltpu.get_barrier_semaphore()
    for peer in (right, left, sibling, beside, across):
        pl.semaphore_signal(barrier, inc=1, device_id=peer, device_id_type=mesh_ids)
    pl.semaphore_wait(barrier, 5)

    def remote(source, target, send, recv, peer):
        copy = pltpu.make_async_remote_copy(
            src_ref=source, dst_ref=target, send_sem=send, recv_sem=recv,
            device_id=peer, device_id_type=mesh_ids)
        copy.start()
        return copy

    onward = (right, left)
    features = kw.shape[0]
    width = kw.shape[1]
    half = width // 2
    cut = features // SUBS
    flight = {}

    def gather_copy(part_id, step, sub, way):
        span = pl.ds(sub * cut, cut)
        if step == 0:
            source = (kw, vw)[way].at[span, pl.ds(part_id * half, half)]
        else:
            source = slots.at[part_id, way, step - 1, span]
        flight[part_id, step, sub, way] = remote(
            source, slots.at[part_id, way, step, span], ag_send.at[part_id, way, step, sub],
            ag_recv.at[part_id, way, step, sub], onward[way])

    for sub in range(SUBS):
        for way in range(2):
            gather_copy(0, 0, sub, way)

    own_rows = hidden.shape[0]
    seq = 2 * own_rows
    strip = 16
    loads[0].wait()

    def normalize(index, carry):
        rows = pl.ds(pl.multiple_of(index * strip, strip), strip)
        wide = hidden[rows, :].astype(jnp.float32)
        inverse = lax.rsqrt(jnp.mean(wide * wide, axis=-1, keepdims=True) + epsilon)
        normed = (wide * inverse * gain[...]).astype(jnp.bfloat16)
        for piece in range(2 * ring):
            stage[piece % 2, piece // 2, rows, :] = normed[:, piece * features:(piece + 1) * features]
        return carry

    lax.fori_loop(0, own_rows // strip, normalize, 0)
    my_rows = pl.ds(pl.multiple_of(core * seq + node * own_rows, own_rows), own_rows)
    act_copies = []
    for relation, (peer, plane) in enumerate(((across, 1 - core), (beside, core), (sibling, 1 - core))):
        act_copies.append(remote(stage.at[plane], act.at[:, my_rows, :], act_send.at[relation],
                                 act_recv.at[relation], peer))
    local_copy = pltpu.make_async_copy(stage.at[core], act.at[:, my_rows, :], act_local)
    local_copy.start()
    for load in loads[1:]:
        load.wait()

    mine = pl.ds(pl.multiple_of(core * seq, seq), seq)
    theirs = pl.ds(pl.multiple_of((1 - core) * seq, seq), seq)
    heads_half = half // HD
    group = HEADS // KV_HEADS
    scale = HD ** (-0.5)
    pairs, swaps = {}, {}
    sum_flight = {}

    def arrived_activations():
        local_copy.wait()
        for copy in act_copies:
            copy.wait_recv()

    def project_own(part_id):
        lanes = slice(part_id * half, (part_id + 1) * half)
        for way in range(2):
            acc[part_id, way] = dot(act[block], own[way, :, lanes])

    def project(part_id, step):
        for way in range(2):
            acc[part_id, way] = acc[part_id, way] + dot(
                act[block_at(position_of(way, step))], slots[part_id, way, step - 1])

    def send_pair(part_id):
        pairs[part_id] = remote(acc.at[part_id, :, theirs, :], part.at[part_id],
                                pair_send.at[part_id], pair_recv.at[part_id], sibling)

    def take_pair(part_id):
        pairs[part_id].wait_recv()
        for kind in range(2):
            total = (acc[part_id, kind, mine, :] + part[part_id, kind]).astype(jnp.bfloat16)
            for head in range(heads_half):
                kv[part_id, kind, head] = total[:, head * HD:(head + 1) * HD]

    key_terms = {}

    def attend(part_id, head, member):
        keys = kv[part_id, 0, head]
        values = kv[part_id, 1, head]
        first = ((part_id * heads_half + head) * group + member) * HD
        lanes = slice(first, first + HD)
        allowed = (lax.broadcasted_iota(jnp.int32, (seq, seq), 0)
                   >= lax.broadcasted_iota(jnp.int32, (seq, seq), 1))
        query = queries[:, lanes]
        scores = jnp.where(allowed, dot_nt(query, keys) * scale, -1e30)
        weights = jnp.exp(scores - jnp.max(scores, axis=-1, keepdims=True))
        probs = (weights / jnp.sum(weights, axis=-1, keepdims=True)).astype(jnp.bfloat16)
        attention[:, lanes] = dot(probs, values).astype(jnp.bfloat16)
        prob_grad = dot_nt(cotangent[:, lanes], values)
        wide = probs.astype(jnp.float32)
        delta = jnp.sum(wide * prob_grad, axis=-1, keepdims=True)
        score_grad = (wide * (prob_grad - delta) * scale).astype(jnp.bfloat16)
        term = dot_tn(score_grad, query)
        if member > 0:
            term = term + key_terms.pop((part_id, head))
        if member < group - 1:
            key_terms[part_id, head] = term
        else:
            rows_grad[part_id, mine, head * HD:(head + 1) * HD] = term.astype(jnp.bfloat16)

    def send_swap(part_id):
        swaps[part_id] = remote(rows_grad.at[part_id, mine], rows_grad.at[part_id, mine],
                                swap_send.at[part_id], swap_recv.at[part_id], sibling)

    share = features // 2
    rows_cut = share // SUBS

    def make_terms(part_id, step):
        for way in range(2):
            position = position_of(way, 1 + step)
            terms[part_id, way] = dot_tn(
                act[block_at(position), :, way * share:(way + 1) * share], rows_grad[part_id])

    def sum_copy(part_id, step, sub, way):
        span = pl.ds(sub * rows_cut, rows_cut)
        sum_flight[part_id, step, sub, way] = remote(
            sums.at[part_id, way, step, span], sums.at[part_id, way, step + 1, span],
            rs_send.at[part_id, way, step, sub], rs_recv.at[part_id, way, step, sub], onward[way])

    def start_sums(part_id):
        swaps[part_id].wait_recv()
        make_terms(part_id, 0)
        for sub in range(SUBS):
            span = slice(sub * rows_cut, (sub + 1) * rows_cut)
            for way in range(2):
                sums[part_id, way, 0, span, :] = terms[part_id, way, span, :]
                sum_copy(part_id, 0, sub, way)
        make_terms(part_id, 1)

    def gather_event(part_id, step, sub):
        for way in range(2):
            flight[part_id, step - 1, sub, way].wait_recv()
            if step < steps:
                gather_copy(part_id, step, sub, way)
            if part_id == 0 and step == steps - 1:
                gather_copy(1, 0, sub, way)

    def sum_event(part_id, step, sub):
        span = slice(sub * rows_cut, (sub + 1) * rows_cut)
        for way in range(2):
            sum_flight[part_id, step - 1, sub, way].wait_recv()
            value = sums[part_id, way, step, span, :] + terms[part_id, way, span, :]
            if step < steps:
                sums[part_id, way, step, span, :] = value
                sum_copy(part_id, step, sub, way)
            else:
                first = way * share + sub * rows_cut
                key_grad[first:first + rows_cut, part_id * half:(part_id + 1) * half] = value
        if sub == SUBS - 1 and step < steps:
            make_terms(part_id, step + 1)

    def attend_tasks(part_id):
        tasks = []
        for head in range(heads_half):
            for member in range(group):
                tasks.append(functools.partial(attend, part_id, head, member))
        first, last = tasks[0], tasks[-1]

        def opening():
            take_pair(part_id)
            first()

        def closing():
            last()
            send_swap(part_id)

        return [opening, *tasks[1:-1], closing]

    def run_events(event, part_id, first, last, tasks):
        for step in range(first, last + 1):
            for sub in range(SUBS):
                event(part_id, step, sub)
                if tasks:
                    tasks.pop(0)()

    run_events(gather_event, 0, 1, steps, [])
    run_events(gather_event, 1, 1, EARLY_B, [])
    arrived_activations()

    def project_first():
        project_own(0)
        for step in range(1, depth):
            project(0, step)

    def project_rest():
        for step in range(depth, steps + 1):
            project(0, step)
        send_pair(0)

    def project_ahead():
        project_own(1)
        for step in range(1, EARLY_B + 1):
            project(1, step)

    tasks = [project_first, project_rest, project_ahead, *attend_tasks(0)]
    tasks.append(functools.partial(start_sums, 0))
    run_events(gather_event, 1, EARLY_B + 1, steps, tasks)
    for task in tasks:
        task()
    for step in range(EARLY_B + 1, steps + 1):
        project(1, step)
    send_pair(1)
    tasks = [lambda: None, *attend_tasks(1), functools.partial(start_sums, 1)]
    run_events(sum_event, 0, 1, steps, tasks)
    for task in tasks:
        task()
    run_events(sum_event, 1, 1, steps, [])
    for copy in [*flight.values(), *act_copies, *pairs.values(), *swaps.values(), *sum_flight.values()]:
        copy.wait_send()


def fused(ring, hidden_in, norm_gain, key_weight, value_weight, queries, out_cotangent):
    features, width = key_weight.shape
    own_rows = hidden_in.shape[0]
    seq = 2 * own_rows
    tokens = 2 * seq
    steps = ring - 1
    half = width // 2
    dma = pltpu.SemaphoreType.DMA
    vmem = pl.BlockSpec(memory_space=pltpu.VMEM)
    anywhere = pl.BlockSpec(memory_space=pl.ANY)
    return pl.pallas_call(
        functools.partial(kernel, ring),
        out_shape=(
            jax.ShapeDtypeStruct(queries.shape, jnp.bfloat16),
            jax.ShapeDtypeStruct((features, width), jnp.float32),
        ),
        in_specs=[anywhere, vmem, anywhere, anywhere, anywhere, anywhere],
        out_specs=(vmem, vmem),
        scratch_shapes=[
            pltpu.VMEM(hidden_in.shape, jnp.bfloat16),
            pltpu.VMEM((2, features, width), jnp.bfloat16),
            pltpu.VMEM(queries.shape, jnp.bfloat16),
            pltpu.VMEM(queries.shape, jnp.bfloat16),
            pltpu.VMEM((2, ring, own_rows, features), jnp.bfloat16),
            pltpu.VMEM((ring, tokens, features), jnp.bfloat16),
            pltpu.VMEM((2, 2, steps, features, half), jnp.bfloat16),
            pltpu.VMEM((2, 2, tokens, half), jnp.float32),
            pltpu.VMEM((2, 2, seq, half), jnp.float32),
            pltpu.VMEM((2, 2, half // HD, seq, HD), jnp.bfloat16),
            pltpu.VMEM((2, tokens, half), jnp.bfloat16),
            pltpu.VMEM((2, 2, ring, features // 2, half), jnp.float32),
            pltpu.VMEM((2, 2, features // 2, half), jnp.float32),
            dma((5,)),
            dma((2, 2, steps, SUBS)),
            dma((2, 2, steps, SUBS)),
            dma((3,)),
            dma((3,)),
            dma,
            dma((2,)),
            dma((2,)),
            dma((2,)),
            dma((2,)),
            dma((2, 2, steps, SUBS)),
            dma((2, 2, steps, SUBS)),
        ],
        compiler_params=pltpu.CompilerParams(
            collective_id=0, has_side_effects=True, vmem_limit_bytes=58 * 1024 * 1024
        ),
        cost_estimate=pl.CostEstimate(flops=4 * 10**9, bytes_accessed=4 * 10**6, transcendentals=0),
    )(hidden_in, norm_gain.reshape(1, -1), key_weight, value_weight, queries, out_cotangent)


def shard_body(mesh, hidden_in, norm_gain, key_weight, value_weight, queries, out_cotangent):
    dp, node = mesh.shape["dp"], mesh.shape["node"]
    features, width = key_weight.shape
    own_rows = hidden_in.shape[0]
    if (
        node == 2
        and dp % 4 == 0
        and EARLY_B + 1 < dp // 2
        and features % 256 == 0
        and width % (4 * HD) == 0
        and own_rows % 16 == 0
        and queries.shape[0] == 2 * own_rows
        and own_rows <= 256
    ):
        return fused(dp // 2, hidden_in, norm_gain, key_weight, value_weight, queries, out_cotangent)
    return local(hidden_in, norm_gain, key_weight, value_weight, queries, out_cotangent)


def solution(mesh):
    in_specs = (
        P(("dp", "node"), None),
        P(),
        P("dp", "node"),
        P("dp", "node"),
        P("dp", "node"),
        P("dp", "node"),
    )
    out_specs = (P("dp", "node"), P("dp", "node"))
    return jax.shard_map(functools.partial(shard_body, mesh), mesh=mesh, in_specs=in_specs, out_specs=out_specs, check_vma=False)
```

```python
import functools

import jax
import jax.numpy as jnp
from jax import lax
from jax.experimental import pallas as pl
from jax.experimental.pallas import tpu as pltpu
from jax.sharding import PartitionSpec as P

HEADS = 16
KV_HEADS = 8
HD = 128


epsilon = 1e-05


def rms_normalize(hidden_rows, norm_gain):
    widened = hidden_rows.astype(jnp.float32)
    inverse = lax.rsqrt(jnp.mean(widened * widened, axis=-1, keepdims=True) + epsilon)
    return (widened * inverse * norm_gain).astype(jnp.bfloat16)


def local(hidden_in, norm_gain, key_weight, value_weight, queries, out_cotangent):
    local_width = key_weight.shape[1]
    kv_local = local_width // HD
    group_size = HEADS // KV_HEADS
    score_scale = HD ** (-0.5)
    gathered = lax.all_gather(hidden_in, "node", axis=0, tiled=True)
    normed = rms_normalize(gathered, norm_gain)
    seq_rows = normed.shape[0]

    def add_rows(shard_piece):
        return jnp.dot(normed, shard_piece, preferred_element_type=jnp.float32)

    key_sum = add_rows(lax.all_gather(key_weight, "dp", axis=0, tiled=True))
    value_sum = add_rows(lax.all_gather(value_weight, "dp", axis=0, tiled=True))
    key_proj = key_sum.astype(jnp.bfloat16).reshape(seq_rows, kv_local, HD)
    value_proj = value_sum.astype(jnp.bfloat16).reshape(seq_rows, kv_local, HD)
    block_rows = min(512, seq_rows)
    outputs = []
    grad_parts = []
    for block_index in range(seq_rows // block_rows):
        row_start = block_index * block_rows
        span_end = row_start + block_rows
        query_block = queries[row_start:span_end].reshape(block_rows, kv_local, group_size, HD)
        grad_block = out_cotangent[row_start:span_end].reshape(block_rows, kv_local, group_size, HD)
        key_window = key_proj[:span_end]
        value_window = value_proj[:span_end]
        scores = (
            jnp.einsum(
                "qkgd,skd->kgqs", query_block, key_window, preferred_element_type=jnp.float32
            )
            * score_scale
        )
        query_pos = row_start + jnp.arange(block_rows, dtype=jnp.int32)
        key_pos = jnp.arange(span_end, dtype=jnp.int32)
        allowed = query_pos[:, None] >= key_pos[None, :]
        scores = jnp.where(allowed, scores, -1e30)
        row_max = jnp.max(scores, axis=-1, keepdims=True)
        weights = jnp.exp(scores - row_max)
        probabilities = (weights / jnp.sum(weights, axis=-1, keepdims=True)).astype(jnp.bfloat16)
        attended = jnp.einsum(
            "kgqs,skd->qkgd", probabilities, value_window, preferred_element_type=jnp.float32
        )
        outputs.append(
            attended.astype(jnp.bfloat16).reshape(block_rows, kv_local * group_size * HD)
        )
        prob_grad = jnp.einsum(
            "qkgd,skd->kgqs", grad_block, value_window, preferred_element_type=jnp.float32
        )
        row_delta = jnp.sum(probabilities * prob_grad, axis=-1, keepdims=True)
        score_grad = (probabilities * (prob_grad - row_delta) * score_scale).astype(jnp.bfloat16)
        block_grad = jnp.einsum(
            "kgqs,qkgd->skd", score_grad, query_block, preferred_element_type=jnp.float32
        )
        grad_parts.append(jnp.pad(block_grad, ((0, seq_rows - span_end), (0, 0), (0, 0))))
    key_grad_acc = grad_parts[0]
    for extra_part in grad_parts[1:]:
        key_grad_acc = key_grad_acc + extra_part
    key_rows_grad = key_grad_acc.reshape(seq_rows, local_width).astype(jnp.bfloat16)
    key_grad = lax.psum_scatter(
        lax.dot_general(
            normed, key_rows_grad, (((0,), (0,)), ((), ())), preferred_element_type=jnp.float32
        ),
        "dp",
        scatter_dimension=0,
        tiled=True,
    )
    return (jnp.concatenate(outputs, axis=0), key_grad)


SUBS = 2
EARLY = 5


def dot(a, b):
    return jnp.dot(a, b, preferred_element_type=jnp.float32)


def dot_nt(a, b):
    return lax.dot_general(a, b, (((1,), (1,)), ((), ())), preferred_element_type=jnp.float32)


def dot_tn(a, b):
    return lax.dot_general(a, b, (((0,), (0,)), ((), ())), preferred_element_type=jnp.float32)


def kernel(ring, hidden_in, gain, kw, vw, queries_in, cotangent_in, attention, key_grad,
           hidden, own, queries, cotangent, stage, act, slots, acc, part, kv, rows_grad, sums,
           in_sem, ag_send, ag_recv, act_send, act_recv, act_local, pair_send, pair_recv,
           rs_send, rs_recv):
    depth = ring // 2
    steps = ring - 1
    dp = lax.axis_index("dp")
    node = lax.axis_index("node")
    core = dp % 2
    block = dp // 2
    col = block % 2
    row = block // 2
    spot = row * (1 - col) + (2 * depth - 1 - row) * col

    def block_at(position):
        position = (position + 2 * ring) % ring
        side = position // depth
        level = position * (1 - side) + (2 * depth - 1 - position) * side
        return level * 2 + side

    right = (block_at(spot + 1) * 2 + core, node)
    left = (block_at(spot - 1) * 2 + core, node)
    sibling = (block * 2 + 1 - core, node)
    beside = (dp, 1 - node)
    across = (block * 2 + 1 - core, 1 - node)
    mesh_ids = pl.DeviceIdType.MESH

    loads = [
        pltpu.make_async_copy(hidden_in, hidden, in_sem.at[0]),
        pltpu.make_async_copy(kw, own.at[0], in_sem.at[1]),
        pltpu.make_async_copy(vw, own.at[1], in_sem.at[2]),
        pltpu.make_async_copy(queries_in, queries, in_sem.at[3]),
        pltpu.make_async_copy(cotangent_in, cotangent, in_sem.at[4]),
    ]
    for load in loads:
        load.start()

    barrier = pltpu.get_barrier_semaphore()
    for peer in (right, left, sibling, beside, across):
        pl.semaphore_signal(barrier, inc=1, device_id=peer, device_id_type=mesh_ids)
    pl.semaphore_wait(barrier, 5)

    def remote(source, target, send, recv, peer):
        copy = pltpu.make_async_remote_copy(
            src_ref=source, dst_ref=target, send_sem=send, recv_sem=recv,
            device_id=peer, device_id_type=mesh_ids)
        copy.start()
        return copy

    onward = (right, left)
    features = kw.shape[0]
    width = kw.shape[1]
    cut = features // SUBS
    started = []

    def gather_copy(way, step, sub):
        span = pl.ds(sub * cut, cut)
        source = (kw, vw)[way].at[span] if step == 0 else slots.at[way, step - 1, span]
        return remote(source, slots.at[way, step, span], ag_send.at[way, step, sub],
                      ag_recv.at[way, step, sub], onward[way])

    flight = {}
    for sub in range(SUBS):
        for way in range(2):
            flight[way, 0, sub] = gather_copy(way, 0, sub)

    own_rows = hidden.shape[0]
    seq = 2 * own_rows
    strip = 16
    loads[0].wait()

    def normalize(index, carry):
        rows = pl.ds(pl.multiple_of(index * strip, strip), strip)
        wide = hidden[rows, :].astype(jnp.float32)
        inverse = lax.rsqrt(jnp.mean(wide * wide, axis=-1, keepdims=True) + epsilon)
        normed = (wide * inverse * gain[...]).astype(jnp.bfloat16)
        for piece in range(2 * ring):
            stage[piece % 2, piece // 2, rows, :] = normed[:, piece * features:(piece + 1) * features]
        return carry

    lax.fori_loop(0, own_rows // strip, normalize, 0)
    my_rows = pl.ds(pl.multiple_of(core * seq + node * own_rows, own_rows), own_rows)
    act_copies = []
    for relation, (peer, plane) in enumerate(((across, 1 - core), (beside, core), (sibling, 1 - core))):
        act_copies.append(remote(stage.at[plane], act.at[:, my_rows, :], act_send.at[relation],
                                 act_recv.at[relation], peer))
    local_copy = pltpu.make_async_copy(stage.at[core], act.at[:, my_rows, :], act_local)
    local_copy.start()
    for load in loads[1:]:
        load.wait()

    def add_block(way, position, weight):
        acc[way] = acc[way] + dot(act[block_at(position)], weight)

    for step in range(1, steps + 1):
        for sub in range(SUBS):
            for way in range(2):
                flight[way, step - 1, sub].wait_recv()
                if step < steps:
                    flight[way, step, sub] = gather_copy(way, step, sub)
        if step == EARLY:
            local_copy.wait()
            for copy in act_copies:
                copy.wait_recv()
            acc[0] = dot(act[block], own[0])
            acc[1] = dot(act[block], own[1])

            def earlier(index, carry):
                add_block(0, spot - 1 - index, slots[0, index])
                add_block(1, spot + 1 + index, slots[1, index])
                return carry

            lax.fori_loop(0, EARLY, earlier, 0)
        if step > EARLY:
            add_block(0, spot - step, slots[0, step - 1])
            add_block(1, spot + step, slots[1, step - 1])

    mine = pl.ds(pl.multiple_of(core * seq, seq), seq)
    theirs = pl.ds(pl.multiple_of((1 - core) * seq, seq), seq)
    pair = remote(acc.at[:, theirs, :], part, pair_send.at[0], pair_recv.at[0], sibling)
    pair.wait_recv()
    kv_heads = width // HD
    group = HEADS // KV_HEADS
    for kind in range(2):
        total = (acc[kind, mine, :] + part[kind]).astype(jnp.bfloat16)
        for head in range(kv_heads):
            kv[kind, head] = total[:, head * HD:(head + 1) * HD]

    scale = HD ** (-0.5)
    allowed = (lax.broadcasted_iota(jnp.int32, (seq, seq), 0)
               >= lax.broadcasted_iota(jnp.int32, (seq, seq), 1))

    def attend(head, carry):
        keys = kv[0, head]
        values = kv[1, head]
        gradient = None
        for member in range(group):
            lanes = pl.ds(pl.multiple_of((head * group + member) * HD, HD), HD)
            query = queries[:, lanes]
            scores = jnp.where(allowed, dot_nt(query, keys) * scale, -1e30)
            weights = jnp.exp(scores - jnp.max(scores, axis=-1, keepdims=True))
            probs = (weights / jnp.sum(weights, axis=-1, keepdims=True)).astype(jnp.bfloat16)
            attention[:, lanes] = dot(probs, values).astype(jnp.bfloat16)
            prob_grad = dot_nt(cotangent[:, lanes], values)
            wide = probs.astype(jnp.float32)
            delta = jnp.sum(wide * prob_grad, axis=-1, keepdims=True)
            score_grad = (wide * (prob_grad - delta) * scale).astype(jnp.bfloat16)
            term = dot_tn(score_grad, query)
            gradient = term if gradient is None else gradient + term
        rows_grad[mine, pl.ds(pl.multiple_of(head * HD, HD), HD)] = gradient.astype(jnp.bfloat16)
        return carry

    lax.fori_loop(0, kv_heads, attend, 0, unroll=True)
    swap = remote(rows_grad.at[mine], rows_grad.at[mine], pair_send.at[1], pair_recv.at[1], sibling)
    swap.wait_recv()

    half = width // 2

    def term_of(way, position):
        return dot_tn(act[block_at(position)], rows_grad[:, way * half:(way + 1) * half])

    ring_flight = {}
    for step in range(steps):
        terms = (term_of(0, spot - 1 - step), term_of(1, spot + 1 + step))
        for sub in range(SUBS):
            span = pl.ds(sub * cut, cut)
            for way in range(2):
                value = terms[way][sub * cut:(sub + 1) * cut]
                if step == 0:
                    sums[way, 0, span, :] = value
                else:
                    ring_flight[way, step - 1, sub].wait_recv()
                    sums[way, step, span, :] = sums[way, step, span, :] + value
                ring_flight[way, step, sub] = remote(
                    sums.at[way, step, span], sums.at[way, step + 1, span],
                    rs_send.at[way, step, sub], rs_recv.at[way, step, sub], onward[way])
    terms = (term_of(0, spot), term_of(1, spot))
    for sub in range(SUBS):
        span = pl.ds(sub * cut, cut)
        for way in range(2):
            ring_flight[way, steps - 1, sub].wait_recv()
            key_grad[span, way * half:(way + 1) * half] = (
                sums[way, steps, span, :] + terms[way][sub * cut:(sub + 1) * cut])
    for copy in [*flight.values(), *act_copies, pair, swap, *ring_flight.values()]:
        copy.wait_send()


def fused(ring, hidden_in, norm_gain, key_weight, value_weight, queries, out_cotangent):
    features, width = key_weight.shape
    own_rows = hidden_in.shape[0]
    seq = 2 * own_rows
    tokens = 2 * seq
    steps = ring - 1
    dma = pltpu.SemaphoreType.DMA
    vmem = pl.BlockSpec(memory_space=pltpu.VMEM)
    anywhere = pl.BlockSpec(memory_space=pl.ANY)
    return pl.pallas_call(
        functools.partial(kernel, ring),
        out_shape=(
            jax.ShapeDtypeStruct(queries.shape, jnp.bfloat16),
            jax.ShapeDtypeStruct((features, width), jnp.float32),
        ),
        in_specs=[anywhere, vmem, anywhere, anywhere, anywhere, anywhere],
        out_specs=(vmem, vmem),
        scratch_shapes=[
            pltpu.VMEM(hidden_in.shape, jnp.bfloat16),
            pltpu.VMEM((2, features, width), jnp.bfloat16),
            pltpu.VMEM(queries.shape, jnp.bfloat16),
            pltpu.VMEM(queries.shape, jnp.bfloat16),
            pltpu.VMEM((2, ring, own_rows, features), jnp.bfloat16),
            pltpu.VMEM((ring, tokens, features), jnp.bfloat16),
            pltpu.VMEM((2, steps, features, width), jnp.bfloat16),
            pltpu.VMEM((2, tokens, width), jnp.float32),
            pltpu.VMEM((2, seq, width), jnp.float32),
            pltpu.VMEM((2, width // HD, seq, HD), jnp.bfloat16),
            pltpu.VMEM((tokens, width), jnp.bfloat16),
            pltpu.VMEM((2, ring, features, width // 2), jnp.float32),
            dma((5,)),
            dma((2, steps, SUBS)),
            dma((2, steps, SUBS)),
            dma((3,)),
            dma((3,)),
            dma,
            dma((2,)),
            dma((2,)),
            dma((2, steps, SUBS)),
            dma((2, steps, SUBS)),
        ],
        compiler_params=pltpu.CompilerParams(
            collective_id=0, has_side_effects=True, vmem_limit_bytes=58 * 1024 * 1024
        ),
        cost_estimate=pl.CostEstimate(flops=4 * 10**9, bytes_accessed=4 * 10**6, transcendentals=0),
    )(hidden_in, norm_gain.reshape(1, -1), key_weight, value_weight, queries, out_cotangent)


def shard_body(mesh, hidden_in, norm_gain, key_weight, value_weight, queries, out_cotangent):
    dp, node = mesh.shape["dp"], mesh.shape["node"]
    features, width = key_weight.shape
    own_rows = hidden_in.shape[0]
    if (
        node == 2
        and dp % 4 == 0
        and EARLY < dp // 2
        and features % 256 == 0
        and width % 256 == 0
        and own_rows % 16 == 0
        and queries.shape[0] == 2 * own_rows
        and own_rows <= 256
    ):
        return fused(dp // 2, hidden_in, norm_gain, key_weight, value_weight, queries, out_cotangent)
    return local(hidden_in, norm_gain, key_weight, value_weight, queries, out_cotangent)


def solution(mesh):
    in_specs = (
        P(("dp", "node"), None),
        P(),
        P("dp", "node"),
        P("dp", "node"),
        P("dp", "node"),
        P("dp", "node"),
    )
    out_specs = (P("dp", "node"), P("dp", "node"))
    return jax.shard_map(functools.partial(shard_body, mesh), mesh=mesh, in_specs=in_specs, out_specs=out_specs, check_vma=False)
```

```python
import functools

import jax
import jax.numpy as jnp
from jax import lax
from jax.experimental import pallas as pl
from jax.experimental.pallas import tpu as pltpu
from jax.sharding import PartitionSpec as P

HEADS = 16
KV_HEADS = 8
HD = 128


epsilon = 1e-05


def rms_normalize(hidden_rows, norm_gain):
    widened = hidden_rows.astype(jnp.float32)
    inverse = lax.rsqrt(jnp.mean(widened * widened, axis=-1, keepdims=True) + epsilon)
    return (widened * inverse * norm_gain).astype(jnp.bfloat16)


def local(hidden_in, norm_gain, key_weight, value_weight, queries, out_cotangent):
    local_width = key_weight.shape[1]
    kv_local = local_width // HD
    group_size = HEADS // KV_HEADS
    score_scale = HD ** (-0.5)
    gathered = lax.all_gather(hidden_in, "node", axis=0, tiled=True)
    normed = rms_normalize(gathered, norm_gain)
    seq_rows = normed.shape[0]

    def add_rows(shard_piece):
        return jnp.dot(normed, shard_piece, preferred_element_type=jnp.float32)

    key_sum = add_rows(lax.all_gather(key_weight, "dp", axis=0, tiled=True))
    value_sum = add_rows(lax.all_gather(value_weight, "dp", axis=0, tiled=True))
    key_proj = key_sum.astype(jnp.bfloat16).reshape(seq_rows, kv_local, HD)
    value_proj = value_sum.astype(jnp.bfloat16).reshape(seq_rows, kv_local, HD)
    block_rows = min(512, seq_rows)
    outputs = []
    grad_parts = []
    for block_index in range(seq_rows // block_rows):
        row_start = block_index * block_rows
        span_end = row_start + block_rows
        query_block = queries[row_start:span_end].reshape(block_rows, kv_local, group_size, HD)
        grad_block = out_cotangent[row_start:span_end].reshape(block_rows, kv_local, group_size, HD)
        key_window = key_proj[:span_end]
        value_window = value_proj[:span_end]
        scores = (
            jnp.einsum(
                "qkgd,skd->kgqs", query_block, key_window, preferred_element_type=jnp.float32
            )
            * score_scale
        )
        query_pos = row_start + jnp.arange(block_rows, dtype=jnp.int32)
        key_pos = jnp.arange(span_end, dtype=jnp.int32)
        allowed = query_pos[:, None] >= key_pos[None, :]
        scores = jnp.where(allowed, scores, -1e30)
        row_max = jnp.max(scores, axis=-1, keepdims=True)
        weights = jnp.exp(scores - row_max)
        probabilities = (weights / jnp.sum(weights, axis=-1, keepdims=True)).astype(jnp.bfloat16)
        attended = jnp.einsum(
            "kgqs,skd->qkgd", probabilities, value_window, preferred_element_type=jnp.float32
        )
        outputs.append(
            attended.astype(jnp.bfloat16).reshape(block_rows, kv_local * group_size * HD)
        )
        prob_grad = jnp.einsum(
            "qkgd,skd->kgqs", grad_block, value_window, preferred_element_type=jnp.float32
        )
        row_delta = jnp.sum(probabilities * prob_grad, axis=-1, keepdims=True)
        score_grad = (probabilities * (prob_grad - row_delta) * score_scale).astype(jnp.bfloat16)
        block_grad = jnp.einsum(
            "kgqs,qkgd->skd", score_grad, query_block, preferred_element_type=jnp.float32
        )
        grad_parts.append(jnp.pad(block_grad, ((0, seq_rows - span_end), (0, 0), (0, 0))))
    key_grad_acc = grad_parts[0]
    for extra_part in grad_parts[1:]:
        key_grad_acc = key_grad_acc + extra_part
    key_rows_grad = key_grad_acc.reshape(seq_rows, local_width).astype(jnp.bfloat16)
    key_grad = lax.psum_scatter(
        lax.dot_general(
            normed, key_rows_grad, (((0,), (0,)), ((), ())), preferred_element_type=jnp.float32
        ),
        "dp",
        scatter_dimension=0,
        tiled=True,
    )
    return (jnp.concatenate(outputs, axis=0), key_grad)


SUBS = 2
EARLY = 5


def dot(a, b):
    return jnp.dot(a, b, preferred_element_type=jnp.float32)


def dot_nt(a, b):
    return lax.dot_general(a, b, (((1,), (1,)), ((), ())), preferred_element_type=jnp.float32)


def dot_tn(a, b):
    return lax.dot_general(a, b, (((0,), (0,)), ((), ())), preferred_element_type=jnp.float32)


def kernel(ring, hidden_in, gain, kw, vw, queries_in, cotangent_in, attention, key_grad,
           hidden, own, queries, cotangent, stage, act, slots, acc, part, kv, rows_grad, sums,
           in_sem, ag_send, ag_recv, act_send, act_recv, act_local, pair_send, pair_recv,
           rs_send, rs_recv):
    depth = ring // 2
    steps = ring - 1
    dp = lax.axis_index("dp")
    node = lax.axis_index("node")
    core = dp % 2
    block = dp // 2
    col = block % 2
    row = block // 2
    spot = row * (1 - col) + (2 * depth - 1 - row) * col

    def block_at(position):
        position = (position + 2 * ring) % ring
        side = position // depth
        level = position * (1 - side) + (2 * depth - 1 - position) * side
        return level * 2 + side

    right = (block_at(spot + 1) * 2 + core, node)
    left = (block_at(spot - 1) * 2 + core, node)
    sibling = (block * 2 + 1 - core, node)
    beside = (dp, 1 - node)
    across = (block * 2 + 1 - core, 1 - node)
    mesh_ids = pl.DeviceIdType.MESH

    loads = [
        pltpu.make_async_copy(hidden_in, hidden, in_sem.at[0]),
        pltpu.make_async_copy(kw, own.at[0], in_sem.at[1]),
        pltpu.make_async_copy(vw, own.at[1], in_sem.at[2]),
        pltpu.make_async_copy(queries_in, queries, in_sem.at[3]),
        pltpu.make_async_copy(cotangent_in, cotangent, in_sem.at[4]),
    ]
    for load in loads:
        load.start()

    barrier = pltpu.get_barrier_semaphore()
    for peer in (right, left, sibling, beside, across):
        pl.semaphore_signal(barrier, inc=1, device_id=peer, device_id_type=mesh_ids)
    pl.semaphore_wait(barrier, 5)

    def remote(source, target, send, recv, peer):
        copy = pltpu.make_async_remote_copy(
            src_ref=source, dst_ref=target, send_sem=send, recv_sem=recv,
            device_id=peer, device_id_type=mesh_ids)
        copy.start()
        return copy

    onward = (right, left)
    features = kw.shape[0]
    width = kw.shape[1]
    cut = features // SUBS
    started = []

    def gather_copy(way, step, sub):
        span = pl.ds(sub * cut, cut)
        source = (kw, vw)[way].at[span] if step == 0 else slots.at[way, step - 1, span]
        return remote(source, slots.at[way, step, span], ag_send.at[way, step, sub],
                      ag_recv.at[way, step, sub], onward[way])

    flight = {}
    for sub in range(SUBS):
        for way in range(2):
            flight[way, 0, sub] = gather_copy(way, 0, sub)

    own_rows = hidden.shape[0]
    seq = 2 * own_rows
    strip = 16
    loads[0].wait()

    def normalize(index, carry):
        rows = pl.ds(pl.multiple_of(index * strip, strip), strip)
        wide = hidden[rows, :].astype(jnp.float32)
        inverse = lax.rsqrt(jnp.mean(wide * wide, axis=-1, keepdims=True) + epsilon)
        normed = (wide * inverse * gain[...]).astype(jnp.bfloat16)
        for piece in range(2 * ring):
            stage[piece % 2, piece // 2, rows, :] = normed[:, piece * features:(piece + 1) * features]
        return carry

    lax.fori_loop(0, own_rows // strip, normalize, 0)
    my_rows = pl.ds(pl.multiple_of(core * seq + node * own_rows, own_rows), own_rows)
    act_copies = []
    for relation, (peer, plane) in enumerate(((across, 1 - core), (beside, core), (sibling, 1 - core))):
        act_copies.append(remote(stage.at[plane], act.at[:, my_rows, :], act_send.at[relation],
                                 act_recv.at[relation], peer))
    local_copy = pltpu.make_async_copy(stage.at[core], act.at[:, my_rows, :], act_local)
    local_copy.start()
    for load in loads[1:]:
        load.wait()

    def add_block(way, position, weight):
        acc[way] = acc[way] + dot(act[block_at(position)], weight)

    for step in range(1, steps + 1):
        for sub in range(SUBS):
            for way in range(2):
                flight[way, step - 1, sub].wait_recv()
                if step < steps:
                    flight[way, step, sub] = gather_copy(way, step, sub)
        if step == EARLY:
            local_copy.wait()
            for copy in act_copies:
                copy.wait_recv()
            acc[0] = dot(act[block], own[0])
            acc[1] = dot(act[block], own[1])

            def earlier(index, carry):
                add_block(0, spot - 1 - index, slots[0, index])
                add_block(1, spot + 1 + index, slots[1, index])
                return carry

            lax.fori_loop(0, EARLY, earlier, 0)
        if EARLY < step < steps:
            add_block(0, spot - step, slots[0, step - 1])
            add_block(1, spot + step, slots[1, step - 1])

    mine = pl.ds(pl.multiple_of(core * seq, seq), seq)
    theirs = pl.ds(pl.multiple_of((1 - core) * seq, seq), seq)
    pairs = []
    for kind, position in enumerate((spot - steps, spot + steps)):
        add_block(kind, position, slots[kind, steps - 1])
        pairs.append(remote(acc.at[kind, theirs, :], part.at[kind], pair_send.at[kind],
                            pair_recv.at[kind], sibling))
    kv_heads = width // HD
    group = HEADS // KV_HEADS
    for kind in range(2):
        pairs[kind].wait_recv()
        total = (acc[kind, mine, :] + part[kind]).astype(jnp.bfloat16)
        for head in range(kv_heads):
            kv[kind, head] = total[:, head * HD:(head + 1) * HD]

    scale = HD ** (-0.5)
    allowed = (lax.broadcasted_iota(jnp.int32, (seq, seq), 0)
               >= lax.broadcasted_iota(jnp.int32, (seq, seq), 1))

    def attend(head, carry):
        keys = kv[0, head]
        values = kv[1, head]
        gradient = None
        for member in range(group):
            lanes = pl.ds(pl.multiple_of((head * group + member) * HD, HD), HD)
            query = queries[:, lanes]
            scores = jnp.where(allowed, dot_nt(query, keys) * scale, -1e30)
            weights = jnp.exp(scores - jnp.max(scores, axis=-1, keepdims=True))
            probs = (weights / jnp.sum(weights, axis=-1, keepdims=True)).astype(jnp.bfloat16)
            attention[:, lanes] = dot(probs, values).astype(jnp.bfloat16)
            prob_grad = dot_nt(cotangent[:, lanes], values)
            wide = probs.astype(jnp.float32)
            delta = jnp.sum(wide * prob_grad, axis=-1, keepdims=True)
            score_grad = (wide * (prob_grad - delta) * scale).astype(jnp.bfloat16)
            term = dot_tn(score_grad, query)
            gradient = term if gradient is None else gradient + term
        rows_grad[mine, pl.ds(pl.multiple_of(head * HD, HD), HD)] = gradient.astype(jnp.bfloat16)
        return carry

    lax.fori_loop(0, kv_heads, attend, 0, unroll=True)
    swap = remote(rows_grad.at[mine], rows_grad.at[mine], pair_send.at[2], pair_recv.at[2], sibling)
    swap.wait_recv()

    half = width // 2

    def term_of(way, position):
        return dot_tn(act[block_at(position)], rows_grad[:, way * half:(way + 1) * half])

    ring_flight = {}
    for step in range(steps):
        terms = (term_of(0, spot - 1 - step), term_of(1, spot + 1 + step))
        for sub in range(SUBS):
            span = pl.ds(sub * cut, cut)
            for way in range(2):
                value = terms[way][sub * cut:(sub + 1) * cut]
                if step == 0:
                    sums[way, 0, span, :] = value
                else:
                    ring_flight[way, step - 1, sub].wait_recv()
                    sums[way, step, span, :] = sums[way, step, span, :] + value
                ring_flight[way, step, sub] = remote(
                    sums.at[way, step, span], sums.at[way, step + 1, span],
                    rs_send.at[way, step, sub], rs_recv.at[way, step, sub], onward[way])
    terms = (term_of(0, spot), term_of(1, spot))
    for sub in range(SUBS):
        span = pl.ds(sub * cut, cut)
        for way in range(2):
            ring_flight[way, steps - 1, sub].wait_recv()
            key_grad[span, way * half:(way + 1) * half] = (
                sums[way, steps, span, :] + terms[way][sub * cut:(sub + 1) * cut])
    for copy in [*flight.values(), *act_copies, *pairs, swap, *ring_flight.values()]:
        copy.wait_send()


def fused(ring, hidden_in, norm_gain, key_weight, value_weight, queries, out_cotangent):
    features, width = key_weight.shape
    own_rows = hidden_in.shape[0]
    seq = 2 * own_rows
    tokens = 2 * seq
    steps = ring - 1
    dma = pltpu.SemaphoreType.DMA
    vmem = pl.BlockSpec(memory_space=pltpu.VMEM)
    anywhere = pl.BlockSpec(memory_space=pl.ANY)
    return pl.pallas_call(
        functools.partial(kernel, ring),
        out_shape=(
            jax.ShapeDtypeStruct(queries.shape, jnp.bfloat16),
            jax.ShapeDtypeStruct((features, width), jnp.float32),
        ),
        in_specs=[anywhere, vmem, anywhere, anywhere, anywhere, anywhere],
        out_specs=(vmem, vmem),
        scratch_shapes=[
            pltpu.VMEM(hidden_in.shape, jnp.bfloat16),
            pltpu.VMEM((2, features, width), jnp.bfloat16),
            pltpu.VMEM(queries.shape, jnp.bfloat16),
            pltpu.VMEM(queries.shape, jnp.bfloat16),
            pltpu.VMEM((2, ring, own_rows, features), jnp.bfloat16),
            pltpu.VMEM((ring, tokens, features), jnp.bfloat16),
            pltpu.VMEM((2, steps, features, width), jnp.bfloat16),
            pltpu.VMEM((2, tokens, width), jnp.float32),
            pltpu.VMEM((2, seq, width), jnp.float32),
            pltpu.VMEM((2, width // HD, seq, HD), jnp.bfloat16),
            pltpu.VMEM((tokens, width), jnp.bfloat16),
            pltpu.VMEM((2, ring, features, width // 2), jnp.float32),
            dma((5,)),
            dma((2, steps, SUBS)),
            dma((2, steps, SUBS)),
            dma((3,)),
            dma((3,)),
            dma,
            dma((3,)),
            dma((3,)),
            dma((2, steps, SUBS)),
            dma((2, steps, SUBS)),
        ],
        compiler_params=pltpu.CompilerParams(
            collective_id=0, has_side_effects=True, vmem_limit_bytes=58 * 1024 * 1024
        ),
        cost_estimate=pl.CostEstimate(flops=4 * 10**9, bytes_accessed=4 * 10**6, transcendentals=0),
    )(hidden_in, norm_gain.reshape(1, -1), key_weight, value_weight, queries, out_cotangent)


def shard_body(mesh, hidden_in, norm_gain, key_weight, value_weight, queries, out_cotangent):
    dp, node = mesh.shape["dp"], mesh.shape["node"]
    features, width = key_weight.shape
    own_rows = hidden_in.shape[0]
    if (
        node == 2
        and dp % 4 == 0
        and EARLY < dp // 2
        and features % 256 == 0
        and width % 256 == 0
        and own_rows % 16 == 0
        and queries.shape[0] == 2 * own_rows
        and own_rows <= 256
    ):
        return fused(dp // 2, hidden_in, norm_gain, key_weight, value_weight, queries, out_cotangent)
    return local(hidden_in, norm_gain, key_weight, value_weight, queries, out_cotangent)


def solution(mesh):
    in_specs = (
        P(("dp", "node"), None),
        P(),
        P("dp", "node"),
        P("dp", "node"),
        P("dp", "node"),
        P("dp", "node"),
    )
    out_specs = (P("dp", "node"), P("dp", "node"))
    return jax.shard_map(functools.partial(shard_body, mesh), mesh=mesh, in_specs=in_specs, out_specs=out_specs, check_vma=False)
```

```python
import functools

import jax
import jax.numpy as jnp
from jax import lax
from jax.experimental import pallas as pl
from jax.experimental.pallas import tpu as pltpu
from jax.sharding import PartitionSpec as P

HEADS = 16
KV_HEADS = 8
HD = 128


epsilon = 1e-05


def rms_normalize(hidden_rows, norm_gain):
    widened = hidden_rows.astype(jnp.float32)
    inverse = lax.rsqrt(jnp.mean(widened * widened, axis=-1, keepdims=True) + epsilon)
    return (widened * inverse * norm_gain).astype(jnp.bfloat16)


def local(hidden_in, norm_gain, key_weight, value_weight, queries, out_cotangent):
    local_width = key_weight.shape[1]
    kv_local = local_width // HD
    group_size = HEADS // KV_HEADS
    score_scale = HD ** (-0.5)
    gathered = lax.all_gather(hidden_in, "node", axis=0, tiled=True)
    normed = rms_normalize(gathered, norm_gain)
    seq_rows = normed.shape[0]

    def add_rows(shard_piece):
        return jnp.dot(normed, shard_piece, preferred_element_type=jnp.float32)

    key_sum = add_rows(lax.all_gather(key_weight, "dp", axis=0, tiled=True))
    value_sum = add_rows(lax.all_gather(value_weight, "dp", axis=0, tiled=True))
    key_proj = key_sum.astype(jnp.bfloat16).reshape(seq_rows, kv_local, HD)
    value_proj = value_sum.astype(jnp.bfloat16).reshape(seq_rows, kv_local, HD)
    block_rows = min(512, seq_rows)
    outputs = []
    grad_parts = []
    for block_index in range(seq_rows // block_rows):
        row_start = block_index * block_rows
        span_end = row_start + block_rows
        query_block = queries[row_start:span_end].reshape(block_rows, kv_local, group_size, HD)
        grad_block = out_cotangent[row_start:span_end].reshape(block_rows, kv_local, group_size, HD)
        key_window = key_proj[:span_end]
        value_window = value_proj[:span_end]
        scores = (
            jnp.einsum(
                "qkgd,skd->kgqs", query_block, key_window, preferred_element_type=jnp.float32
            )
            * score_scale
        )
        query_pos = row_start + jnp.arange(block_rows, dtype=jnp.int32)
        key_pos = jnp.arange(span_end, dtype=jnp.int32)
        allowed = query_pos[:, None] >= key_pos[None, :]
        scores = jnp.where(allowed, scores, -1e30)
        row_max = jnp.max(scores, axis=-1, keepdims=True)
        weights = jnp.exp(scores - row_max)
        probabilities = (weights / jnp.sum(weights, axis=-1, keepdims=True)).astype(jnp.bfloat16)
        attended = jnp.einsum(
            "kgqs,skd->qkgd", probabilities, value_window, preferred_element_type=jnp.float32
        )
        outputs.append(
            attended.astype(jnp.bfloat16).reshape(block_rows, kv_local * group_size * HD)
        )
        prob_grad = jnp.einsum(
            "qkgd,skd->kgqs", grad_block, value_window, preferred_element_type=jnp.float32
        )
        row_delta = jnp.sum(probabilities * prob_grad, axis=-1, keepdims=True)
        score_grad = (probabilities * (prob_grad - row_delta) * score_scale).astype(jnp.bfloat16)
        block_grad = jnp.einsum(
            "kgqs,qkgd->skd", score_grad, query_block, preferred_element_type=jnp.float32
        )
        grad_parts.append(jnp.pad(block_grad, ((0, seq_rows - span_end), (0, 0), (0, 0))))
    key_grad_acc = grad_parts[0]
    for extra_part in grad_parts[1:]:
        key_grad_acc = key_grad_acc + extra_part
    key_rows_grad = key_grad_acc.reshape(seq_rows, local_width).astype(jnp.bfloat16)
    key_grad = lax.psum_scatter(
        lax.dot_general(
            normed, key_rows_grad, (((0,), (0,)), ((), ())), preferred_element_type=jnp.float32
        ),
        "dp",
        scatter_dimension=0,
        tiled=True,
    )
    return (jnp.concatenate(outputs, axis=0), key_grad)


SUBS = 1
EARLY = 5


def dot(a, b):
    return jnp.dot(a, b, preferred_element_type=jnp.float32)


def dot_nt(a, b):
    return lax.dot_general(a, b, (((1,), (1,)), ((), ())), preferred_element_type=jnp.float32)


def dot_tn(a, b):
    return lax.dot_general(a, b, (((0,), (0,)), ((), ())), preferred_element_type=jnp.float32)


def kernel(ring, hidden_in, gain, kw, vw, queries_in, cotangent_in, attention, key_grad,
           hidden, own, queries, cotangent, stage, act, slots, acc, part, kv, rows_grad, sums, terms,
           in_sem, ag_send, ag_recv, act_send, act_recv, act_local, pair_send, pair_recv,
           swap_send, swap_recv, rs_send, rs_recv):
    depth = ring // 2
    steps = ring - 1
    dp = lax.axis_index("dp")
    node = lax.axis_index("node")
    core = dp % 2
    block = dp // 2
    col = block % 2
    row = block // 2
    spot = row * (1 - col) + (2 * depth - 1 - row) * col

    def block_at(position):
        position = (position + 2 * ring) % ring
        side = position // depth
        level = position * (1 - side) + (2 * depth - 1 - position) * side
        return level * 2 + side

    def position_of(way, step):
        return spot - step if way == 0 else spot + step

    right = (block_at(spot + 1) * 2 + core, node)
    left = (block_at(spot - 1) * 2 + core, node)
    sibling = (block * 2 + 1 - core, node)
    beside = (dp, 1 - node)
    across = (block * 2 + 1 - core, 1 - node)
    mesh_ids = pl.DeviceIdType.MESH

    loads = [
        pltpu.make_async_copy(hidden_in, hidden, in_sem.at[0]),
        pltpu.make_async_copy(kw, own.at[0], in_sem.at[1]),
        pltpu.make_async_copy(vw, own.at[1], in_sem.at[2]),
        pltpu.make_async_copy(queries_in, queries, in_sem.at[3]),
        pltpu.make_async_copy(cotangent_in, cotangent, in_sem.at[4]),
    ]
    for load in loads:
        load.start()

    barrier = pltpu.get_barrier_semaphore()
    for peer in (right, left, sibling, beside, across):
        pl.semaphore_signal(barrier, inc=1, device_id=peer, device_id_type=mesh_ids)
    pl.semaphore_wait(barrier, 5)

    def remote(source, target, send, recv, peer):
        copy = pltpu.make_async_remote_copy(
            src_ref=source, dst_ref=target, send_sem=send, recv_sem=recv,
            device_id=peer, device_id_type=mesh_ids)
        copy.start()
        return copy

    onward = (right, left)
    features = kw.shape[0]
    width = kw.shape[1]
    half = width // 2
    cut = features // SUBS
    flight = {}

    def gather_copy(part_id, step, sub, way):
        span = pl.ds(sub * cut, cut)
        if step == 0:
            source = (kw, vw)[way].at[span, pl.ds(part_id * half, half)]
        else:
            source = slots.at[part_id, way, step - 1, span]
        flight[part_id, step, sub, way] = remote(
            source, slots.at[part_id, way, step, span], ag_send.at[part_id, way, step, sub],
            ag_recv.at[part_id, way, step, sub], onward[way])

    for part_id in range(2):
        for way in range(2):
            gather_copy(part_id, 0, 0, way)

    own_rows = hidden.shape[0]
    seq = 2 * own_rows
    strip = 16
    loads[0].wait()

    def normalize(index, carry):
        rows = pl.ds(pl.multiple_of(index * strip, strip), strip)
        wide = hidden[rows, :].astype(jnp.float32)
        inverse = lax.rsqrt(jnp.mean(wide * wide, axis=-1, keepdims=True) + epsilon)
        normed = (wide * inverse * gain[...]).astype(jnp.bfloat16)
        for piece in range(2 * ring):
            stage[piece % 2, piece // 2, rows, :] = normed[:, piece * features:(piece + 1) * features]
        return carry

    lax.fori_loop(0, own_rows // strip, normalize, 0)
    my_rows = pl.ds(pl.multiple_of(core * seq + node * own_rows, own_rows), own_rows)
    act_copies = []
    for relation, (peer, plane) in enumerate(((across, 1 - core), (beside, core), (sibling, 1 - core))):
        act_copies.append(remote(stage.at[plane], act.at[:, my_rows, :], act_send.at[relation],
                                 act_recv.at[relation], peer))
    local_copy = pltpu.make_async_copy(stage.at[core], act.at[:, my_rows, :], act_local)
    local_copy.start()
    for load in loads[1:]:
        load.wait()

    mine = pl.ds(pl.multiple_of(core * seq, seq), seq)
    theirs = pl.ds(pl.multiple_of((1 - core) * seq, seq), seq)
    heads_half = half // HD
    group = HEADS // KV_HEADS
    scale = HD ** (-0.5)
    pairs, swaps = {}, {}
    sum_flight = {}

    def arrived_activations():
        local_copy.wait()
        for copy in act_copies:
            copy.wait_recv()

    def project_own(part_id):
        lanes = slice(part_id * half, (part_id + 1) * half)
        for way in range(2):
            acc[part_id, way] = dot(act[block], own[way, :, lanes])

    def project(part_id, step):
        for way in range(2):
            acc[part_id, way] = acc[part_id, way] + dot(
                act[block_at(position_of(way, step))], slots[part_id, way, step - 1])

    def send_pair(part_id):
        pairs[part_id] = remote(acc.at[part_id, :, theirs, :], part.at[part_id],
                                pair_send.at[part_id], pair_recv.at[part_id], sibling)

    def take_pair(part_id):
        pairs[part_id].wait_recv()
        for kind in range(2):
            total = (acc[part_id, kind, mine, :] + part[part_id, kind]).astype(jnp.bfloat16)
            for head in range(heads_half):
                kv[part_id, kind, head] = total[:, head * HD:(head + 1) * HD]

    key_terms = {}

    def attend(part_id, head, member):
        keys = kv[part_id, 0, head]
        values = kv[part_id, 1, head]
        first = ((part_id * heads_half + head) * group + member) * HD
        lanes = slice(first, first + HD)
        allowed = (lax.broadcasted_iota(jnp.int32, (seq, seq), 0)
                   >= lax.broadcasted_iota(jnp.int32, (seq, seq), 1))
        query = queries[:, lanes]
        scores = jnp.where(allowed, dot_nt(query, keys) * scale, -1e30)
        weights = jnp.exp(scores - jnp.max(scores, axis=-1, keepdims=True))
        probs = (weights / jnp.sum(weights, axis=-1, keepdims=True)).astype(jnp.bfloat16)
        attention[:, lanes] = dot(probs, values).astype(jnp.bfloat16)
        prob_grad = dot_nt(cotangent[:, lanes], values)
        wide = probs.astype(jnp.float32)
        delta = jnp.sum(wide * prob_grad, axis=-1, keepdims=True)
        score_grad = (wide * (prob_grad - delta) * scale).astype(jnp.bfloat16)
        term = dot_tn(score_grad, query)
        if member > 0:
            term = term + key_terms.pop((part_id, head))
        if member < group - 1:
            key_terms[part_id, head] = term
        else:
            rows_grad[part_id, mine, head * HD:(head + 1) * HD] = term.astype(jnp.bfloat16)

    def send_swap(part_id):
        swaps[part_id] = remote(rows_grad.at[part_id, mine], rows_grad.at[part_id, mine],
                                swap_send.at[part_id], swap_recv.at[part_id], sibling)

    share = features // 2
    rows_cut = share // SUBS

    def make_terms(part_id, step):
        for way in range(2):
            position = position_of(way, 1 + step)
            terms[part_id, way] = dot_tn(
                act[block_at(position), :, way * share:(way + 1) * share], rows_grad[part_id])

    def sum_copy(part_id, step, sub, way):
        span = pl.ds(sub * rows_cut, rows_cut)
        sum_flight[part_id, step, sub, way] = remote(
            sums.at[part_id, way, step, span], sums.at[part_id, way, step + 1, span],
            rs_send.at[part_id, way, step, sub], rs_recv.at[part_id, way, step, sub], onward[way])

    def start_sums(part_id):
        swaps[part_id].wait_recv()
        make_terms(part_id, 0)
        for sub in range(SUBS):
            span = slice(sub * rows_cut, (sub + 1) * rows_cut)
            for way in range(2):
                sums[part_id, way, 0, span, :] = terms[part_id, way, span, :]
                sum_copy(part_id, 0, sub, way)
        make_terms(part_id, 1)

    def gather_event(part_id, step, sub):
        for way in range(2):
            flight[part_id, step - 1, sub, way].wait_recv()
            if step < steps:
                gather_copy(part_id, step, sub, way)

    def sum_event(part_id, step, sub):
        span = slice(sub * rows_cut, (sub + 1) * rows_cut)
        for way in range(2):
            sum_flight[part_id, step - 1, sub, way].wait_recv()
            value = sums[part_id, way, step, span, :] + terms[part_id, way, span, :]
            if step < steps:
                sums[part_id, way, step, span, :] = value
                sum_copy(part_id, step, sub, way)
            else:
                first = way * share + sub * rows_cut
                key_grad[first:first + rows_cut, part_id * half:(part_id + 1) * half] = value
        if sub == SUBS - 1 and step < steps:
            make_terms(part_id, step + 1)

    def attend_tasks(part_id):
        tasks = []
        for head in range(heads_half):
            for member in range(group):
                tasks.append(functools.partial(attend, part_id, head, member))
        first, last = tasks[0], tasks[-1]

        def opening():
            take_pair(part_id)
            first()

        def closing():
            last()
            send_swap(part_id)

        return [opening, *tasks[1:-1], closing]

    def own_first():
        arrived_activations()
        project_own(0)
        project_own(1)

    work = [own_first]
    for step in range(1, steps - 1):
        for part_id in range(2):
            work.append(functools.partial(project, part_id, step))
    for step in range(1, steps):
        for part_id in range(2):
            gather_event(part_id, step, 0)
            if step >= EARLY:
                for _ in range(3):
                    if work:
                        work.pop(0)()
    for task in work:
        task()
    for part_id in range(2):
        project(part_id, steps - 1)
    for part_id in range(2):
        gather_event(part_id, steps, 0)
        project(part_id, steps)
        send_pair(part_id)
    for task in attend_tasks(0):
        task()
    second = attend_tasks(1)
    second[0]()
    start_sums(0)
    for task in second[1:]:
        task()
    start_sums(1)
    for step in range(1, steps + 1):
        for part_id in range(2):
            sum_event(part_id, step, 0)
    for copy in [*flight.values(), *act_copies, *pairs.values(), *swaps.values(), *sum_flight.values()]:
        copy.wait_send()


def fused(ring, hidden_in, norm_gain, key_weight, value_weight, queries, out_cotangent):
    features, width = key_weight.shape
    own_rows = hidden_in.shape[0]
    seq = 2 * own_rows
    tokens = 2 * seq
    steps = ring - 1
    half = width // 2
    dma = pltpu.SemaphoreType.DMA
    vmem = pl.BlockSpec(memory_space=pltpu.VMEM)
    anywhere = pl.BlockSpec(memory_space=pl.ANY)
    return pl.pallas_call(
        functools.partial(kernel, ring),
        out_shape=(
            jax.ShapeDtypeStruct(queries.shape, jnp.bfloat16),
            jax.ShapeDtypeStruct((features, width), jnp.float32),
        ),
        in_specs=[anywhere, vmem, anywhere, anywhere, anywhere, anywhere],
        out_specs=(vmem, vmem),
        scratch_shapes=[
            pltpu.VMEM(hidden_in.shape, jnp.bfloat16),
            pltpu.VMEM((2, features, width), jnp.bfloat16),
            pltpu.VMEM(queries.shape, jnp.bfloat16),
            pltpu.VMEM(queries.shape, jnp.bfloat16),
            pltpu.VMEM((2, ring, own_rows, features), jnp.bfloat16),
            pltpu.VMEM((ring, tokens, features), jnp.bfloat16),
            pltpu.VMEM((2, 2, steps, features, half), jnp.bfloat16),
            pltpu.VMEM((2, 2, tokens, half), jnp.float32),
            pltpu.VMEM((2, 2, seq, half), jnp.float32),
            pltpu.VMEM((2, 2, half // HD, seq, HD), jnp.bfloat16),
            pltpu.VMEM((2, tokens, half), jnp.bfloat16),
            pltpu.VMEM((2, 2, ring, features // 2, half), jnp.float32),
            pltpu.VMEM((2, 2, features // 2, half), jnp.float32),
            dma((5,)),
            dma((2, 2, steps, SUBS)),
            dma((2, 2, steps, SUBS)),
            dma((3,)),
            dma((3,)),
            dma,
            dma((2,)),
            dma((2,)),
            dma((2,)),
            dma((2,)),
            dma((2, 2, steps, SUBS)),
            dma((2, 2, steps, SUBS)),
        ],
        compiler_params=pltpu.CompilerParams(
            collective_id=0, has_side_effects=True, vmem_limit_bytes=58 * 1024 * 1024
        ),
        cost_estimate=pl.CostEstimate(flops=4 * 10**9, bytes_accessed=4 * 10**6, transcendentals=0),
    )(hidden_in, norm_gain.reshape(1, -1), key_weight, value_weight, queries, out_cotangent)


def shard_body(mesh, hidden_in, norm_gain, key_weight, value_weight, queries, out_cotangent):
    dp, node = mesh.shape["dp"], mesh.shape["node"]
    features, width = key_weight.shape
    own_rows = hidden_in.shape[0]
    if (
        node == 2
        and dp % 4 == 0
        and EARLY + 2 < dp // 2
        and features % 256 == 0
        and width % (4 * HD) == 0
        and own_rows % 16 == 0
        and queries.shape[0] == 2 * own_rows
        and own_rows <= 256
    ):
        return fused(dp // 2, hidden_in, norm_gain, key_weight, value_weight, queries, out_cotangent)
    return local(hidden_in, norm_gain, key_weight, value_weight, queries, out_cotangent)


def solution(mesh):
    in_specs = (
        P(("dp", "node"), None),
        P(),
        P("dp", "node"),
        P("dp", "node"),
        P("dp", "node"),
        P("dp", "node"),
    )
    out_specs = (P("dp", "node"), P("dp", "node"))
    return jax.shard_map(functools.partial(shard_body, mesh), mesh=mesh, in_specs=in_specs, out_specs=out_specs, check_vma=False)
```

```python
import functools

import jax
import jax.numpy as jnp
from jax import lax
from jax.experimental import pallas as pl
from jax.experimental.pallas import tpu as pltpu
from jax.sharding import PartitionSpec as P

HEADS = 16
KV_HEADS = 8
HD = 128


epsilon = 1e-05


def rms_normalize(hidden_rows, norm_gain):
    widened = hidden_rows.astype(jnp.float32)
    inverse = lax.rsqrt(jnp.mean(widened * widened, axis=-1, keepdims=True) + epsilon)
    return (widened * inverse * norm_gain).astype(jnp.bfloat16)


def local(hidden_in, norm_gain, key_weight, value_weight, queries, out_cotangent):
    local_width = key_weight.shape[1]
    kv_local = local_width // HD
    group_size = HEADS // KV_HEADS
    score_scale = HD ** (-0.5)
    gathered = lax.all_gather(hidden_in, "node", axis=0, tiled=True)
    normed = rms_normalize(gathered, norm_gain)
    seq_rows = normed.shape[0]

    def add_rows(shard_piece):
        return jnp.dot(normed, shard_piece, preferred_element_type=jnp.float32)

    key_sum = add_rows(lax.all_gather(key_weight, "dp", axis=0, tiled=True))
    value_sum = add_rows(lax.all_gather(value_weight, "dp", axis=0, tiled=True))
    key_proj = key_sum.astype(jnp.bfloat16).reshape(seq_rows, kv_local, HD)
    value_proj = value_sum.astype(jnp.bfloat16).reshape(seq_rows, kv_local, HD)
    block_rows = min(512, seq_rows)
    outputs = []
    grad_parts = []
    for block_index in range(seq_rows // block_rows):
        row_start = block_index * block_rows
        span_end = row_start + block_rows
        query_block = queries[row_start:span_end].reshape(block_rows, kv_local, group_size, HD)
        grad_block = out_cotangent[row_start:span_end].reshape(block_rows, kv_local, group_size, HD)
        key_window = key_proj[:span_end]
        value_window = value_proj[:span_end]
        scores = (
            jnp.einsum(
                "qkgd,skd->kgqs", query_block, key_window, preferred_element_type=jnp.float32
            )
            * score_scale
        )
        query_pos = row_start + jnp.arange(block_rows, dtype=jnp.int32)
        key_pos = jnp.arange(span_end, dtype=jnp.int32)
        allowed = query_pos[:, None] >= key_pos[None, :]
        scores = jnp.where(allowed, scores, -1e30)
        row_max = jnp.max(scores, axis=-1, keepdims=True)
        weights = jnp.exp(scores - row_max)
        probabilities = (weights / jnp.sum(weights, axis=-1, keepdims=True)).astype(jnp.bfloat16)
        attended = jnp.einsum(
            "kgqs,skd->qkgd", probabilities, value_window, preferred_element_type=jnp.float32
        )
        outputs.append(
            attended.astype(jnp.bfloat16).reshape(block_rows, kv_local * group_size * HD)
        )
        prob_grad = jnp.einsum(
            "qkgd,skd->kgqs", grad_block, value_window, preferred_element_type=jnp.float32
        )
        row_delta = jnp.sum(probabilities * prob_grad, axis=-1, keepdims=True)
        score_grad = (probabilities * (prob_grad - row_delta) * score_scale).astype(jnp.bfloat16)
        block_grad = jnp.einsum(
            "kgqs,qkgd->skd", score_grad, query_block, preferred_element_type=jnp.float32
        )
        grad_parts.append(jnp.pad(block_grad, ((0, seq_rows - span_end), (0, 0), (0, 0))))
    key_grad_acc = grad_parts[0]
    for extra_part in grad_parts[1:]:
        key_grad_acc = key_grad_acc + extra_part
    key_rows_grad = key_grad_acc.reshape(seq_rows, local_width).astype(jnp.bfloat16)
    key_grad = lax.psum_scatter(
        lax.dot_general(
            normed, key_rows_grad, (((0,), (0,)), ((), ())), preferred_element_type=jnp.float32
        ),
        "dp",
        scatter_dimension=0,
        tiled=True,
    )
    return (jnp.concatenate(outputs, axis=0), key_grad)


SUBS = 1
EARLY = 5


def dot(a, b):
    return jnp.dot(a, b, preferred_element_type=jnp.float32)


def dot_nt(a, b):
    return lax.dot_general(a, b, (((1,), (1,)), ((), ())), preferred_element_type=jnp.float32)


def dot_tn(a, b):
    return lax.dot_general(a, b, (((0,), (0,)), ((), ())), preferred_element_type=jnp.float32)


def kernel(ring, hidden_in, gain_in, kw, vw, queries_in, cotangent_in, attention, key_grad,
           hidden, gain, own, queries, cotangent, stage, act, slots, acc, part, kv, rows_grad, sums, terms,
           in_sem, ag_send, ag_recv, act_send, act_recv, act_local, pair_send, pair_recv,
           swap_send, swap_recv, rs_send, rs_recv):
    depth = ring // 2
    steps = ring - 1
    dp = lax.axis_index("dp")
    node = lax.axis_index("node")
    core = dp % 2
    block = dp // 2
    col = block % 2
    row = block // 2
    spot = row * (1 - col) + (2 * depth - 1 - row) * col

    def block_at(position):
        position = (position + 2 * ring) % ring
        side = position // depth
        level = position * (1 - side) + (2 * depth - 1 - position) * side
        return level * 2 + side

    def position_of(way, step):
        return spot - step if way == 0 else spot + step

    right = (block_at(spot + 1) * 2 + core, node)
    left = (block_at(spot - 1) * 2 + core, node)
    sibling = (block * 2 + 1 - core, node)
    beside = (dp, 1 - node)
    across = (block * 2 + 1 - core, 1 - node)
    mesh_ids = pl.DeviceIdType.MESH

    loads = [
        pltpu.make_async_copy(hidden_in, hidden, in_sem.at[0]),
        pltpu.make_async_copy(kw, own.at[0], in_sem.at[1]),
        pltpu.make_async_copy(vw, own.at[1], in_sem.at[2]),
        pltpu.make_async_copy(queries_in, queries, in_sem.at[3]),
        pltpu.make_async_copy(cotangent_in, cotangent, in_sem.at[4]),
        pltpu.make_async_copy(gain_in, gain, in_sem.at[5]),
    ]
    for load in loads:
        load.start()

    barrier = pltpu.get_barrier_semaphore()
    for peer in (right, left, sibling, beside, across):
        pl.semaphore_signal(barrier, inc=1, device_id=peer, device_id_type=mesh_ids)
    pl.semaphore_wait(barrier, 5)

    def remote(source, target, send, recv, peer):
        copy = pltpu.make_async_remote_copy(
            src_ref=source, dst_ref=target, send_sem=send, recv_sem=recv,
            device_id=peer, device_id_type=mesh_ids)
        copy.start()
        return copy

    onward = (right, left)
    features = kw.shape[0]
    width = kw.shape[1]
    half = width // 2
    cut = features // SUBS
    flight = {}

    def gather_copy(part_id, step, sub, way):
        span = pl.ds(sub * cut, cut)
        if step == 0:
            source = (kw, vw)[way].at[span, pl.ds(part_id * half, half)]
        else:
            source = slots.at[part_id, way, step - 1, span]
        flight[part_id, step, sub, way] = remote(
            source, slots.at[part_id, way, step, span], ag_send.at[part_id, way, step, sub],
            ag_recv.at[part_id, way, step, sub], onward[way])

    for part_id in range(2):
        for way in range(2):
            gather_copy(part_id, 0, 0, way)

    own_rows = hidden.shape[0]
    seq = 2 * own_rows
    strip = 16
    loads[0].wait()
    loads[5].wait()

    def normalize(index, carry):
        rows = pl.ds(pl.multiple_of(index * strip, strip), strip)
        wide = hidden[rows, :].astype(jnp.float32)
        inverse = lax.rsqrt(jnp.mean(wide * wide, axis=-1, keepdims=True) + epsilon)
        normed = (wide * inverse * gain[...]).astype(jnp.bfloat16)
        for piece in range(2 * ring):
            stage[piece % 2, piece // 2, rows, :] = normed[:, piece * features:(piece + 1) * features]
        return carry

    lax.fori_loop(0, own_rows // strip, normalize, 0)
    my_rows = pl.ds(pl.multiple_of(core * seq + node * own_rows, own_rows), own_rows)
    act_copies = []
    for relation, (peer, plane) in enumerate(((across, 1 - core), (beside, core), (sibling, 1 - core))):
        act_copies.append(remote(stage.at[plane], act.at[:, my_rows, :], act_send.at[relation],
                                 act_recv.at[relation], peer))
    local_copy = pltpu.make_async_copy(stage.at[core], act.at[:, my_rows, :], act_local)
    local_copy.start()
    for load in loads[1:5]:
        load.wait()

    mine = pl.ds(pl.multiple_of(core * seq, seq), seq)
    theirs = pl.ds(pl.multiple_of((1 - core) * seq, seq), seq)
    heads_half = half // HD
    group = HEADS // KV_HEADS
    scale = HD ** (-0.5)
    pairs, swaps = {}, {}
    sum_flight = {}

    def arrived_activations():
        local_copy.wait()
        for copy in act_copies:
            copy.wait_recv()

    def project_own(part_id):
        lanes = slice(part_id * half, (part_id + 1) * half)
        for way in range(2):
            acc[part_id, way] = dot(act[block], own[way, :, lanes])

    def project(part_id, step):
        for way in range(2):
            acc[part_id, way] = acc[part_id, way] + dot(
                act[block_at(position_of(way, step))], slots[part_id, way, step - 1])

    def send_pair(part_id):
        pairs[part_id] = remote(acc.at[part_id, :, theirs, :], part.at[part_id],
                                pair_send.at[part_id], pair_recv.at[part_id], sibling)

    def take_pair(part_id):
        pairs[part_id].wait_recv()
        for kind in range(2):
            total = (acc[part_id, kind, mine, :] + part[part_id, kind]).astype(jnp.bfloat16)
            for head in range(heads_half):
                kv[part_id, kind, head] = total[:, head * HD:(head + 1) * HD]

    key_terms = {}

    def attend(part_id, head, member):
        keys = kv[part_id, 0, head]
        values = kv[part_id, 1, head]
        first = ((part_id * heads_half + head) * group + member) * HD
        lanes = slice(first, first + HD)
        allowed = (lax.broadcasted_iota(jnp.int32, (seq, seq), 0)
                   >= lax.broadcasted_iota(jnp.int32, (seq, seq), 1))
        query = queries[:, lanes]
        scores = jnp.where(allowed, dot_nt(query, keys) * scale, -1e30)
        weights = jnp.exp(scores - jnp.max(scores, axis=-1, keepdims=True))
        probs = (weights / jnp.sum(weights, axis=-1, keepdims=True)).astype(jnp.bfloat16)
        attention[:, lanes] = dot(probs, values).astype(jnp.bfloat16)
        prob_grad = dot_nt(cotangent[:, lanes], values)
        wide = probs.astype(jnp.float32)
        delta = jnp.sum(wide * prob_grad, axis=-1, keepdims=True)
        score_grad = (wide * (prob_grad - delta) * scale).astype(jnp.bfloat16)
        term = dot_tn(score_grad, query)
        if member > 0:
            term = term + key_terms.pop((part_id, head))
        if member < group - 1:
            key_terms[part_id, head] = term
        else:
            rows_grad[part_id, mine, head * HD:(head + 1) * HD] = term.astype(jnp.bfloat16)

    def send_swap(part_id):
        swaps[part_id] = remote(rows_grad.at[part_id, mine], rows_grad.at[part_id, mine],
                                swap_send.at[part_id], swap_recv.at[part_id], sibling)

    share = features // 2
    rows_cut = share // SUBS

    def make_terms(part_id, step):
        for way in range(2):
            position = position_of(way, 1 + step)
            terms[part_id, way] = dot_tn(
                act[block_at(position), :, way * share:(way + 1) * share], rows_grad[part_id])

    def sum_copy(part_id, step, sub, way):
        span = pl.ds(sub * rows_cut, rows_cut)
        sum_flight[part_id, step, sub, way] = remote(
            sums.at[part_id, way, step, span], sums.at[part_id, way, step + 1, span],
            rs_send.at[part_id, way, step, sub], rs_recv.at[part_id, way, step, sub], onward[way])

    def start_sums(part_id):
        swaps[part_id].wait_recv()
        make_terms(part_id, 0)
        for sub in range(SUBS):
            span = slice(sub * rows_cut, (sub + 1) * rows_cut)
            for way in range(2):
                sums[part_id, way, 0, span, :] = terms[part_id, way, span, :]
                sum_copy(part_id, 0, sub, way)
        make_terms(part_id, 1)

    def gather_event(part_id, step, sub):
        for way in range(2):
            flight[part_id, step - 1, sub, way].wait_recv()
            if step < steps:
                gather_copy(part_id, step, sub, way)

    def sum_event(part_id, step, sub):
        span = slice(sub * rows_cut, (sub + 1) * rows_cut)
        for way in range(2):
            sum_flight[part_id, step - 1, sub, way].wait_recv()
            value = sums[part_id, way, step, span, :] + terms[part_id, way, span, :]
            if step < steps:
                sums[part_id, way, step, span, :] = value
                sum_copy(part_id, step, sub, way)
            else:
                first = way * share + sub * rows_cut
                key_grad[first:first + rows_cut, part_id * half:(part_id + 1) * half] = value
        if sub == SUBS - 1 and step < steps:
            make_terms(part_id, step + 1)

    def attend_tasks(part_id):
        tasks = []
        for head in range(heads_half):
            for member in range(group):
                tasks.append(functools.partial(attend, part_id, head, member))
        first, last = tasks[0], tasks[-1]

        def opening():
            take_pair(part_id)
            first()

        def closing():
            last()
            send_swap(part_id)

        return [opening, *tasks[1:-1], closing]

    def own_first():
        arrived_activations()
        project_own(0)
        project_own(1)

    work = [own_first]
    for step in range(1, steps - 1):
        for part_id in range(2):
            work.append(functools.partial(project, part_id, step))
    for step in range(1, steps):
        for part_id in range(2):
            gather_event(part_id, step, 0)
            if step >= EARLY:
                for _ in range(3):
                    if work:
                        work.pop(0)()
    for task in work:
        task()
    for part_id in range(2):
        project(part_id, steps - 1)
    for part_id in range(2):
        gather_event(part_id, steps, 0)
        project(part_id, steps)
        send_pair(part_id)
    for task in attend_tasks(0):
        task()
    second = attend_tasks(1)
    second[0]()
    start_sums(0)
    for task in second[1:]:
        task()
    start_sums(1)
    for step in range(1, steps + 1):
        for part_id in range(2):
            sum_event(part_id, step, 0)
    for copy in [*flight.values(), *act_copies, *pairs.values(), *swaps.values(), *sum_flight.values()]:
        copy.wait_send()


def fused(ring, hidden_in, norm_gain, key_weight, value_weight, queries, out_cotangent):
    features, width = key_weight.shape
    own_rows = hidden_in.shape[0]
    seq = 2 * own_rows
    tokens = 2 * seq
    steps = ring - 1
    half = width // 2
    dma = pltpu.SemaphoreType.DMA
    vmem = pl.BlockSpec(memory_space=pltpu.VMEM)
    anywhere = pl.BlockSpec(memory_space=pl.ANY)
    return pl.pallas_call(
        functools.partial(kernel, ring),
        out_shape=(
            jax.ShapeDtypeStruct(queries.shape, jnp.bfloat16),
            jax.ShapeDtypeStruct((features, width), jnp.float32),
        ),
        in_specs=[anywhere] * 6,
        out_specs=(vmem, vmem),
        scratch_shapes=[
            pltpu.VMEM(hidden_in.shape, jnp.bfloat16),
            pltpu.VMEM((1, hidden_in.shape[1]), jnp.float32),
            pltpu.VMEM((2, features, width), jnp.bfloat16),
            pltpu.VMEM(queries.shape, jnp.bfloat16),
            pltpu.VMEM(queries.shape, jnp.bfloat16),
            pltpu.VMEM((2, ring, own_rows, features), jnp.bfloat16),
            pltpu.VMEM((ring, tokens, features), jnp.bfloat16),
            pltpu.VMEM((2, 2, steps, features, half), jnp.bfloat16),
            pltpu.VMEM((2, 2, tokens, half), jnp.float32),
            pltpu.VMEM((2, 2, seq, half), jnp.float32),
            pltpu.VMEM((2, 2, half // HD, seq, HD), jnp.bfloat16),
            pltpu.VMEM((2, tokens, half), jnp.bfloat16),
            pltpu.VMEM((2, 2, ring, features // 2, half), jnp.float32),
            pltpu.VMEM((2, 2, features // 2, half), jnp.float32),
            dma((6,)),
            dma((2, 2, steps, SUBS)),
            dma((2, 2, steps, SUBS)),
            dma((3,)),
            dma((3,)),
            dma,
            dma((2,)),
            dma((2,)),
            dma((2,)),
            dma((2,)),
            dma((2, 2, steps, SUBS)),
            dma((2, 2, steps, SUBS)),
        ],
        compiler_params=pltpu.CompilerParams(
            collective_id=0, has_side_effects=True, vmem_limit_bytes=58 * 1024 * 1024
        ),
        cost_estimate=pl.CostEstimate(flops=4 * 10**9, bytes_accessed=4 * 10**6, transcendentals=0),
    )(hidden_in, norm_gain.reshape(1, -1), key_weight, value_weight, queries, out_cotangent)


def shard_body(mesh, hidden_in, norm_gain, key_weight, value_weight, queries, out_cotangent):
    dp, node = mesh.shape["dp"], mesh.shape["node"]
    features, width = key_weight.shape
    own_rows = hidden_in.shape[0]
    if (
        node == 2
        and dp % 4 == 0
        and EARLY + 2 < dp // 2
        and features % 256 == 0
        and width % (4 * HD) == 0
        and own_rows % 16 == 0
        and queries.shape[0] == 2 * own_rows
        and own_rows <= 256
    ):
        return fused(dp // 2, hidden_in, norm_gain, key_weight, value_weight, queries, out_cotangent)
    return local(hidden_in, norm_gain, key_weight, value_weight, queries, out_cotangent)


def solution(mesh):
    in_specs = (
        P(("dp", "node"), None),
        P(),
        P("dp", "node"),
        P("dp", "node"),
        P("dp", "node"),
        P("dp", "node"),
    )
    out_specs = (P("dp", "node"), P("dp", "node"))
    return jax.shard_map(functools.partial(shard_body, mesh), mesh=mesh, in_specs=in_specs, out_specs=out_specs, check_vma=False)
```
